256 devices in a mesh: inst: 8 (over y, core), tp: 32 (over z, x).
Axes of the slice: x: 4, y: 4, z: 8, core: 2. Of those that a mesh axis runs over, the one named last changes fastest.
Arguments:
- queries: bfloat16 [2, 64, 8192], P(None, 'inst', 'tp'), may hold values from -32 to 32
- new_keys: bfloat16 [2, 64, 1024], P(None, 'inst'), may hold values from -6 to 6
- new_values: bfloat16 [2, 64, 1024], P(None, 'inst'), may hold values from -6 to 6
- k_cache: bfloat16 [4096, 128, 1024], P(('inst', 'tp')), may hold values from -4 to 4
- v_cache: bfloat16 [4096, 128, 1024], P(('inst', 'tp')), may hold values from -6 to 6
- block_req: int32 [4096], P(('inst', 'tp')), may hold values from 0 to 63
- block_fill: int32 [4096], P(('inst', 'tp')), may hold values from 1 to 128
Outputs:
- attended: bfloat16 [2, 64, 8192], P(None, 'inst', 'tp')
The draws below stay inside these ranges and needn't reach their ends.
All inputs are finite; a program needn't handle non-finite values.
Results may differ from the reference program's by a relative error of at most 0.0041.
Values may be sent and summed in bfloat16 or wider, within the bound.
No kernel may reach another device: no remote copies, remote signals or barrier semaphores. Data moves between devices by JAX's collectives and lax.ppermute only.
A program may use at most 64 MiB of HBM per device.

```python
import math
import jax
import jax.numpy as jnp
import numpy as np
from jax import lax

H = 64
KVH = 8
DH = 128
BLK = 128
STEPS = 2
SLOTS = 16
R = 64
BLOCKS = 4096
N_INST = 8
N_TP = 32


def draw_queries(key, part):
    key = jax.random.fold_in(key, 1)
    drawn = jnp.clip(jax.random.normal(key, (STEPS, R, H, DH), jnp.float32), -6.0, 6.0)
    return drawn.reshape(STEPS, R, H * DH).astype(jnp.bfloat16)


def draw_k_cache(key, part):
    key = jax.random.fold_in(key, 2)
    drawn = jnp.clip(jax.random.normal(key, (BLOCKS, BLK, KVH, DH), jnp.float32), -4.0, 4.0)
    return drawn.reshape(BLOCKS, BLK, KVH * DH).astype(jnp.bfloat16)


def with_ends(values, rng, smallest, top_value):
    extent = values.shape
    index_at = [jax.random.randint(jax.random.fold_in(rng, axis), (), 0, extent[axis]) for axis in range(len(extent))]
    values = values.at[tuple(index_at)].set(smallest)
    longest = extent.index(max(extent))
    index_at[longest] = (index_at[longest] + 1) % extent[longest]
    return values.at[tuple(index_at)].set(top_value)


def levels(key, shape, cuts, least, largest):
    level = 1.0
    for position, shards_of in cuts:
        steps = jax.random.uniform(jax.random.fold_in(jax.random.fold_in(key, 6), position), (shards_of,), jnp.float32, least / len(cuts), largest / len(cuts))
        level = level * jnp.repeat(jnp.exp(steps), shape[position] // shards_of).reshape((-1,) + (1,) * (len(shape) - 1 - position))
    return level


def rank_table(count, lean):
    loads = [(1 << 20) // math.isqrt(rank ** lean) + 1 for rank in range(1, count + 1)]
    deviation = 1 + sum(loads) // (1 << 30)
    return np.cumsum(np.array([max(1, weight // deviation) for weight in loads]))


def ranked_ids(stream_key, shape, amount, slope):
    table = rank_table(amount, slope)
    pick = jax.random.randint(jax.random.fold_in(stream_key, 1), shape, 0, int(table[amount - 1]))
    standing = jnp.searchsorted(jnp.asarray(table, jnp.int32), pick, side="right")
    return jax.random.permutation(jax.random.fold_in(stream_key, 2), amount)[standing].astype(jnp.int32)


def normal_values(key, dims, spread, reach, shards=(), kind=jnp.bfloat16):
    factor_of = levels(key, dims, shards, -0.22, 0.18) if shards else 1.0
    array = jax.random.normal(key, dims, jnp.float32) * spread * factor_of
    return jnp.minimum(jnp.maximum(array, -reach), reach).astype(kind)


def setup_inputs(seed: int = 0) -> dict:
    splits = jax.random.split(jax.random.key(seed), 8)
    return {
        "queries": draw_queries(jax.random.fold_in(splits[7], 71), 0),
        "new_keys": normal_values(splits[1], (STEPS, R, KVH * DH), 1.0, 6.0, ((1, 8),)),
        "new_values": normal_values(splits[2], (STEPS, R, KVH * DH), 1.0, 6.0, ((1, 8),)),
        "k_cache": draw_k_cache(jax.random.fold_in(splits[7], 71), 0),
        "v_cache": normal_values(splits[4], (BLOCKS, BLK, KVH * DH), 1.0, 6.0, ((0, 256),)),
        "block_req": with_ends(ranked_ids(splits[5], (BLOCKS,), R, 2), jax.random.fold_in(splits[5], 3), 0, R - 1).astype(jnp.int32),
        "block_fill": with_ends(jax.random.randint(splits[6], (BLOCKS,), 1, BLK + 1), jax.random.fold_in(splits[6], 1), 1, BLK).astype(jnp.int32),
    }


far_below = -1.0e30


def block_terms(queries, keys, values, owners, fills):
    n_steps = queries.shape[0]
    block_count = keys.shape[0]
    per_kv = H // KVH
    picked = queries[:, owners].astype(jnp.float32).reshape(n_steps, block_count, KVH, per_kv, DH)
    keys_f = keys.astype(jnp.float32).reshape(block_count, BLK, KVH, DH)
    scores = jnp.einsum("sbgqd,btgd->sbgqt", picked, keys_f, precision=lax.Precision.HIGHEST) * (DH ** -0.5)
    in_block = jnp.arange(BLK, dtype=jnp.int32)[None, :] < fills[:, None]
    scores = jnp.where(in_block[None, :, None, None, :], scores, far_below)
    highest = jnp.max(scores, axis=-1)
    chances = jnp.exp(scores - highest[..., None])
    totals = jnp.sum(chances, axis=-1)
    rounded = lax.optimization_barrier(chances.astype(jnp.bfloat16)).astype(jnp.float32)
    values_f = values.astype(jnp.float32).reshape(block_count, BLK, KVH, DH)
    mixed_out = jnp.einsum("sbgqt,btgd->sbgqd", rounded, values_f, precision=lax.Precision.HIGHEST)
    return (highest.reshape(n_steps, block_count, H), totals.reshape(n_steps, block_count, H),
            mixed_out.reshape(n_steps, block_count, H, DH))


def finish(own_q, new_keys, new_values, peak_own, numerators, denominators, kv_index):
    n_steps = own_q.shape[0]
    own_rows = own_q.shape[1]
    own_heads = kv_index.shape[0]
    query_f = own_q.astype(jnp.float32).reshape(n_steps, own_rows, own_heads, DH)
    keys_f = jnp.take(new_keys.astype(jnp.float32).reshape(n_steps, own_rows, KVH, DH), kv_index, axis=2)
    values_f = jnp.take(new_values.astype(jnp.float32).reshape(n_steps, own_rows, KVH, DH), kv_index, axis=2)
    fresh_scores = jnp.einsum("srhd,jrhd->sjrh", query_f, keys_f, precision=lax.Precision.HIGHEST) * (DH ** -0.5)
    causal = jnp.arange(n_steps, dtype=jnp.int32)[None, :] <= jnp.arange(n_steps, dtype=jnp.int32)[:, None]
    fresh_scores = jnp.where(causal[:, :, None, None], fresh_scores, far_below)
    highest = jnp.maximum(peak_own, jnp.max(fresh_scores, axis=1))
    retain = jnp.exp(peak_own - highest)
    fresh_w = jnp.exp(fresh_scores - highest[:, None])
    numerator = numerators * retain[..., None] + jnp.sum(fresh_w[..., None] * values_f[None], axis=1)
    denominator = denominators * retain + jnp.sum(fresh_w, axis=1)
    return (numerator / denominator[..., None]).reshape(n_steps, own_rows, own_heads * DH).astype(jnp.bfloat16)


def reference(queries, new_keys, new_values, k_cache, v_cache, block_req, block_fill):
    devices = N_INST * N_TP
    n_steps = queries.shape[0]

    def per_device(device_items):
        return block_terms(queries, device_items[0], device_items[1], device_items[2], device_items[3])

    highest, totals, mixed_out = lax.map(per_device, (
        k_cache.reshape(devices, SLOTS, BLK, KVH * DH),
        v_cache.reshape(devices, SLOTS, BLK, KVH * DH),
        block_req.reshape(devices, SLOTS),
        block_fill.reshape(devices, SLOTS)))
    highest = jnp.moveaxis(highest, 0, 1).reshape(n_steps, BLOCKS, H)
    totals = jnp.moveaxis(totals, 0, 1).reshape(n_steps, BLOCKS, H)
    mixed_out = jnp.moveaxis(mixed_out, 0, 1).reshape(n_steps, BLOCKS, H, DH)
    owner_hot = block_req[None, :] == jnp.arange(R, dtype=jnp.int32)[:, None]
    request_peak = jnp.max(jnp.where(owner_hot[None, :, :, None], highest[:, None, :, :], far_below), axis=2)
    factor = jnp.exp(highest - request_peak[:, block_req])
    hot_f = owner_hot.astype(jnp.float32)
    numerators = jnp.einsum("rb,sbhd->srhd", hot_f, mixed_out * factor[..., None], precision=lax.Precision.HIGHEST)
    denominators = jnp.einsum("rb,sbh->srh", hot_f, totals * factor, precision=lax.Precision.HIGHEST)
    kv_index = jnp.arange(H, dtype=jnp.int32) // (H // KVH)
    return finish(queries, new_keys, new_values, request_peak, numerators, denominators, kv_index)
```

```python
import jax
import jax.numpy as jnp
from jax import lax
from jax.experimental import pallas as pl
from jax.experimental.pallas import tpu as pltpu
from jax.sharding import Mesh, PartitionSpec as P

H = 64
KVH = 8
DH = 128
BLK = 128
SCALE = DH ** (-0.5)

far_below = -1e30


def split_three(x):
    hi = x.astype(jnp.bfloat16)
    rest = x - hi.astype(jnp.float32)
    mid = rest.astype(jnp.bfloat16)
    lo = (rest - mid.astype(jnp.float32)).astype(jnp.bfloat16)
    return hi, mid, lo


def lay_kernel(here, *refs):
    pieces, out_ref, ordered = refs[:-2], refs[-2], refs[-1]
    for m, piece in enumerate(pieces):
        ordered[here[0] ^ m] = piece[...]
    for z in range(out_ref.shape[0]):
        out_ref[z] = jnp.concatenate([ordered[x, z] for x in range(len(pieces))], axis=1)


def lay(here, pieces):
    n_z, rows, depth, width = pieces[0].shape
    return pl.pallas_call(
        lay_kernel,
        out_shape=jax.ShapeDtypeStruct((n_z, rows, len(pieces) * depth, width), pieces[0].dtype),
        in_specs=[pl.BlockSpec(memory_space=pltpu.SMEM)]
        + [pl.BlockSpec(memory_space=pltpu.VMEM)] * len(pieces),
        out_specs=pl.BlockSpec(memory_space=pltpu.VMEM),
        scratch_shapes=[pltpu.VMEM((len(pieces), n_z, rows, depth, width), pieces[0].dtype)],
        name="lay",
    )(here, *pieces)


def block_kernel(here, owner, fill, k_hbm, v_hbm, *refs):
    pieces = refs[:-6]
    out_ref, k_all, v_all, picked, stats, sem = refs[-6:]
    slots, n_kv, per, _ = picked.shape
    cols = n_kv * per
    n_tp = out_ref.shape[0]
    together = 8
    rows = pieces[0].shape[1]
    n_core = 2
    n_y = len(pieces) // n_core

    def fetch(b):
        home = owner[b] // rows
        row = lax.rem(owner[b], rows)
        which = (home // n_core ^ here[0]) + (lax.rem(home, n_core) ^ here[1]) * n_y
        for p, piece in enumerate(pieces):

            @pl.when(which == p)
            def _(piece=piece):
                pltpu.make_async_copy(piece.at[:, row], picked.at[b], sem.at[2, b]).start()

    def copies(b):
        return (
            pltpu.make_async_copy(k_hbm.at[b], k_all.at[b], sem.at[0, b]),
            pltpu.make_async_copy(v_hbm.at[b], v_all.at[b], sem.at[1, b]),
        )

    def start(b, _):
        fetch(b)
        for c in copies(b):
            c.start()
        return 0

    lax.fori_loop(0, slots, start, 0)
    stats[...] = jnp.zeros_like(stats)
    slot_at = lax.broadcasted_iota(jnp.int32, (BLK, cols), 0)
    nothing = jnp.zeros((per, DH), jnp.bfloat16)

    def score(b):
        spread = []
        for g in range(n_kv):
            mine = picked[b, g]
            spread.append(
                jnp.concatenate([nothing] * g + [mine] + [nothing] * (n_kv - 1 - g), axis=1)
            )
        scores = lax.dot_general(
            k_all[b],
            jnp.concatenate(spread, axis=0),
            (((1,), (1,)), ((), ())),
            preferred_element_type=jnp.float32,
        )
        return jnp.where(slot_at < fill[b], scores * SCALE, far_below)

    def soften(b, scores):
        peak = jnp.max(scores, axis=0, keepdims=True)
        chances = jnp.exp(scores - peak)
        total = jnp.sum(chances, axis=0, keepdims=True)
        for p, piece in enumerate(split_three(peak) + split_three(total)):
            stats[pl.ds(p * slots + b, 1)] = piece.astype(jnp.float32)
        stats[pl.ds(6 * slots + b, 1)] = jnp.broadcast_to(owner[b].astype(jnp.float32), (1, cols))
        return chances.astype(jnp.bfloat16).T

    def mix(b, rounded):
        mixed = []
        for g in range(n_kv):
            mixed.append(
                jnp.dot(
                    rounded[g * per : (g + 1) * per],
                    v_all[b, :, g * DH : (g + 1) * DH],
                    preferred_element_type=jnp.float32,
                ).astype(jnp.bfloat16)
            )
        mixed = jnp.concatenate(mixed, axis=0)
        out_ref[:, pl.ds(b, 1)] = mixed.reshape(n_tp, 1, cols // n_tp, DH)

    def some_blocks(i, _):
        first = i * together
        for j in range(together):
            for c in copies(first + j):
                c.wait()
            pltpu.make_async_copy(pieces[0].at[:, 0], picked.at[first + j], sem.at[2, first + j]).wait()
        scores = [score(first + j) for j in range(together)]
        rounded = [soften(first + j, scores[j]) for j in range(together)]
        for j in range(together):
            mix(first + j, rounded[j])
        return 0

    lax.fori_loop(0, slots // together, some_blocks, 0)
    packed = stats[...].T.astype(jnp.bfloat16)
    out_ref[:, pl.ds(slots, 1)] = packed.reshape(n_tp, 1, cols // n_tp, DH)


def blocks(here, pieces, k_cache, v_cache, block_req, block_fill, n_tp):
    slots = k_cache.shape[0]
    n_kv, _, per, _ = pieces[0].shape
    cols = n_kv * per
    return pl.pallas_call(
        block_kernel,
        out_shape=jax.ShapeDtypeStruct((n_tp, slots + 1, cols // n_tp, DH), jnp.bfloat16),
        in_specs=[pl.BlockSpec(memory_space=pltpu.SMEM)] * 3
        + [pl.BlockSpec(memory_space=pl.ANY)] * (2 + len(pieces)),
        out_specs=pl.BlockSpec(memory_space=pltpu.VMEM),
        scratch_shapes=[
            pltpu.VMEM(k_cache.shape, k_cache.dtype),
            pltpu.VMEM(v_cache.shape, v_cache.dtype),
            pltpu.VMEM((slots, n_kv, per, DH), pieces[0].dtype),
            pltpu.VMEM((DH, cols), jnp.float32),
            pltpu.SemaphoreType.DMA((3, slots)),
        ],
        compiler_params=pltpu.CompilerParams(vmem_limit_bytes=56 * 1024 * 1024),
        cost_estimate=pl.CostEstimate(
            flops=4 * slots * BLK * DH * 128, bytes_accessed=9 * 1024 * 1024, transcendentals=slots * BLK * 128
        ),
        name="blocks",
    )(here, block_req, block_fill, k_cache, v_cache, *pieces)


def combine(got, requests):
    n_src = got.shape[0]
    slots = got.shape[1] - 1
    n_cols = got.shape[2]
    out = got[:, :slots].reshape(n_src * slots, n_cols, DH)
    stats = got[:, slots, :, : 7 * slots].astype(jnp.float32)
    stats = stats.reshape(n_src, n_cols, 7, slots).transpose(2, 1, 0, 3)
    stats = stats.reshape(7, n_cols, n_src * slots)
    peak = stats[0] + stats[1] + stats[2]
    total = stats[3] + stats[4] + stats[5]
    owner = stats[6, 0].astype(jnp.int32)
    hot = owner[None, :] == jnp.arange(requests, dtype=jnp.int32)[:, None]
    masked = jnp.where(hot[None], peak[:, None, :], far_below)
    top = jnp.max(masked, axis=-1, keepdims=True)
    weight = jnp.where(hot[None], jnp.exp(masked - top), 0.0)
    den = jnp.sum(weight * total[:, None], axis=-1, keepdims=True)
    w_hi = lax.reduce_precision(weight, 8, 7)
    w_lo = (weight - w_hi).astype(jnp.bfloat16)
    w_hi = w_hi.astype(jnp.bfloat16)
    num = jnp.einsum("crj,jcd->crd", w_hi, out, preferred_element_type=jnp.float32) + jnp.einsum(
        "crj,jcd->crd", w_lo, out, preferred_element_type=jnp.float32
    )
    some = den > 0.0
    safe = jnp.where(some, den, 1.0)
    return num / safe, jnp.where(some, top + jnp.log(safe), far_below)


def fresh_kernel(q_ref, keys_ref, values_ref, out_ref):
    n_steps, own_rows, width = q_ref.shape
    n_heads = width // DH
    lane = lax.broadcasted_iota(jnp.int32, (own_rows, DH), 1)
    levels = jnp.zeros((own_rows, DH), jnp.float32)
    for s in range(n_steps):
        for h in range(n_heads):
            c = s * n_heads + h
            query = q_ref[s, :, h * DH : (h + 1) * DH].astype(jnp.float32)
            fresh = [
                jnp.sum(query * keys_ref[j].astype(jnp.float32), axis=1, keepdims=True) * SCALE
                for j in range(s + 1)
            ]
            top = fresh[0]
            for x in fresh[1:]:
                top = jnp.maximum(top, x)
            num = jnp.zeros((own_rows, DH), jnp.float32)
            den = jnp.zeros((own_rows, 1), jnp.float32)
            for j in range(s + 1):
                weight = jnp.exp(fresh[j] - top)
                num = num + weight * values_ref[j].astype(jnp.float32)
                den = den + weight
            out_ref[c] = num / den
            levels = jnp.where(lane == c, top + jnp.log(den), levels)
    out_ref[n_steps * n_heads] = levels


def fresh_part(queries, keys, values):
    n_steps, own_rows, width = queries.shape
    return pl.pallas_call(
        fresh_kernel,
        out_shape=jax.ShapeDtypeStruct((n_steps * (width // DH) + 1, own_rows, DH), jnp.float32),
        in_specs=[pl.BlockSpec(memory_space=pltpu.VMEM)] * 3,
        out_specs=pl.BlockSpec(memory_space=pltpu.VMEM),
        cost_estimate=pl.CostEstimate(flops=1 << 17, bytes_accessed=1 << 16, transcendentals=1 << 8),
        name="fresh",
    )(queries, keys, values)


def finish_kernel(got, fresh, out_ref):
    n_steps, own_rows, width = out_ref.shape
    n_heads = width // DH
    last = n_steps * n_heads
    parts = [got.at[i] for i in range(got.shape[0])] + [fresh]
    levels = [part[last] for part in parts]
    top = levels[0]
    for x in levels[1:]:
        top = jnp.maximum(top, x)
    weights = [jnp.exp(x - top) for x in levels]
    den = weights[0]
    for x in weights[1:]:
        den = den + x
    inverse = 1.0 / den
    weights = [x * inverse for x in weights]
    for s in range(n_steps):
        for h in range(n_heads):
            c = s * n_heads + h
            num = jnp.zeros((own_rows, DH), jnp.float32)
            for weight, part in zip(weights, parts):
                num = num + weight[:, c : c + 1] * part[c]
            out_ref[s, :, h * DH : (h + 1) * DH] = num.astype(out_ref.dtype)


def finish(got, fresh, n_steps):
    own_rows = got.shape[2]
    width = (got.shape[1] - 1) // n_steps * DH
    return pl.pallas_call(
        finish_kernel,
        out_shape=jax.ShapeDtypeStruct((n_steps, own_rows, width), jnp.bfloat16),
        in_specs=[pl.BlockSpec(memory_space=pltpu.VMEM)] * 2,
        out_specs=pl.BlockSpec(memory_space=pltpu.VMEM),
        name="finish",
    )(got, fresh)


def body(queries, new_keys, new_values, k_cache, v_cache, block_req, block_fill):
    n_steps, own_rows, width = queries.shape
    own_heads = width // DH
    n_y, n_core = lax.axis_size("y"), lax.axis_size("core")
    n_z, n_x = lax.axis_size("z"), lax.axis_size("x")
    n_inst = n_y * n_core

    def from_other(value, axis, m):
        return lax.ppermute(value, axis, [(j, j ^ m) for j in range(lax.axis_size(axis))])

    rows = queries.reshape(n_steps, own_rows, own_heads, DH).transpose(1, 0, 2, 3)
    rows = rows.reshape(own_rows, n_steps * own_heads, DH)
    rows = lax.all_to_all(
        jnp.broadcast_to(rows[None], (n_z,) + rows.shape), "z", 0, 0, tiled=True
    )
    at_x = lax.axis_index("x").astype(jnp.int32).reshape(1)
    own = lay(at_x, [rows] + [from_other(rows, "x", m) for m in range(1, n_x)])
    at_kv = lax.axis_index("z") * DH
    keys = lax.dynamic_slice_in_dim(new_keys, at_kv, DH, axis=2)
    values = lax.dynamic_slice_in_dim(new_values, at_kv, DH, axis=2)
    own, keys, values = lax.optimization_barrier((own, keys, values))
    pieces = [own] + [from_other(own, "y", m) for m in range(1, n_y)]
    pieces = pieces + [from_other(p, "core", 1) for p in pieces]
    here = jnp.stack([lax.axis_index("y"), lax.axis_index("core")]).astype(jnp.int32)
    sent = blocks(here, pieces, k_cache, v_cache, block_req, block_fill, n_z * n_x)
    sent, keys, values = lax.optimization_barrier((sent, keys, values))
    got = lax.all_to_all(sent, ("z", "x"), split_axis=0, concat_axis=0, tiled=True)
    got, fresh = lax.optimization_barrier((got, fresh_part(queries, keys, values)))
    part, level = combine(got, n_inst * own_rows)
    level = level[..., 0].reshape(4, n_inst, own_rows).transpose(1, 2, 0)
    level = jnp.pad(level, ((0, 0), (0, 0), (0, DH - 4)))[:, None]
    part = part.reshape(4, n_inst, own_rows, DH).transpose(1, 0, 2, 3)
    both = lax.all_to_all(
        jnp.concatenate([part, level], axis=1), ("y", "core"), 0, 0, tiled=True
    )
    return finish(both, fresh, n_steps)


def solution(mesh):
    n_inst, n_tp = mesh.devices.shape
    split = Mesh(
        mesh.devices.reshape(n_inst // 2, 2, KVH, n_tp // KVH), ("y", "core", "z", "x")
    )
    inst, tp = ("y", "core"), ("z", "x")
    return jax.shard_map(
        body,
        mesh=split,
        in_specs=(
            P(None, inst, tp),
            P(None, inst, None),
            P(None, inst, None),
            P(inst + tp, None, None),
            P(inst + tp, None, None),
            P(inst + tp),
            P(inst + tp),
        ),
        out_specs=P(None, inst, tp),
        check_vma=False,
    )
```

```python
import jax
import jax.numpy as jnp
from jax import lax
from jax.experimental import pallas as pl
from jax.experimental.pallas import tpu as pltpu
from jax.sharding import Mesh, PartitionSpec as P

H = 64
KVH = 8
DH = 128
BLK = 128
SCALE = DH ** (-0.5)

far_below = -1e30


def split_three(x):
    hi = x.astype(jnp.bfloat16)
    rest = x - hi.astype(jnp.float32)
    mid = rest.astype(jnp.bfloat16)
    lo = (rest - mid.astype(jnp.float32)).astype(jnp.bfloat16)
    return hi, mid, lo


def block_kernel(owner, fill, k_hbm, v_hbm, *refs):
    pieces = refs[:-6]
    out_ref, k_all, v_all, picked, stats, sem = refs[-6:]
    slots, n_tp, depth, _ = picked.shape
    cols = n_tp * depth
    n_kv = KVH
    per, n_x = cols // n_kv, n_tp // n_kv
    together = 4
    rows = pieces[0].shape[1]
    n_core = 2
    n_y = len(pieces) // n_core
    here_y, here_core = lax.axis_index("y"), lax.axis_index("core")

    def fetch(b):
        home = owner[b] // rows
        row = lax.rem(owner[b], rows)
        which = (home // n_core ^ here_y) + (lax.rem(home, n_core) ^ here_core) * n_y
        for p, piece in enumerate(pieces):

            @pl.when(which == p)
            def _(piece=piece):
                pltpu.make_async_copy(piece.at[:, row], picked.at[b], sem.at[2, b]).start()

    def copies(b):
        return (
            pltpu.make_async_copy(k_hbm.at[b], k_all.at[b], sem.at[0, b]),
            pltpu.make_async_copy(v_hbm.at[b], v_all.at[b], sem.at[1, b]),
        )

    def start(b, _):
        fetch(b)
        for c in copies(b):
            c.start()
        return 0

    lax.fori_loop(0, slots, start, 0)
    stats[...] = jnp.zeros_like(stats)
    slot_at = lax.broadcasted_iota(jnp.int32, (BLK, cols), 0)
    nothing = jnp.zeros((per, DH), jnp.bfloat16)

    def score(b):
        spread = []
        for g in range(n_kv):
            mine = picked[b, g * n_x : (g + 1) * n_x].reshape(per, DH)
            spread.append(
                jnp.concatenate([nothing] * g + [mine] + [nothing] * (n_kv - 1 - g), axis=1)
            )
        scores = lax.dot_general(
            k_all[b],
            jnp.concatenate(spread, axis=0),
            (((1,), (1,)), ((), ())),
            preferred_element_type=jnp.float32,
        )
        return jnp.where(slot_at < fill[b], scores * SCALE, far_below)

    def soften(b, scores):
        peak = jnp.max(scores, axis=0, keepdims=True)
        chances = jnp.exp(scores - peak)
        total = jnp.sum(chances, axis=0, keepdims=True)
        for p, piece in enumerate(split_three(peak) + split_three(total)):
            stats[pl.ds(p * slots + b, 1)] = piece.astype(jnp.float32)
        stats[pl.ds(6 * slots + b, 1)] = jnp.broadcast_to(owner[b].astype(jnp.float32), (1, cols))
        return chances.astype(jnp.bfloat16).T

    def mix(b, rounded):
        mixed = []
        for g in range(0, n_kv, 2):
            two = jnp.dot(
                rounded[g * per : (g + 2) * per],
                v_all[b, :, g * DH : (g + 2) * DH],
                preferred_element_type=jnp.float32,
            ).astype(jnp.bfloat16)
            mixed = mixed + [two[:per, :DH], two[per:, DH:]]
        mixed = jnp.concatenate(mixed, axis=0)
        out_ref[:, pl.ds(b, 1)] = mixed.reshape(n_tp, 1, cols // n_tp, DH)

    def some_blocks(i, _):
        first = i * together
        for j in range(together):
            for c in copies(first + j):
                c.wait()
            pltpu.make_async_copy(pieces[0].at[:, 0], picked.at[first + j], sem.at[2, first + j]).wait()
        scores = [score(first + j) for j in range(together)]
        rounded = [soften(first + j, scores[j]) for j in range(together)]
        for j in range(together):
            mix(first + j, rounded[j])
        return 0

    lax.fori_loop(0, slots // together, some_blocks, 0)
    packed = stats[...].T.astype(jnp.bfloat16)
    out_ref[:, pl.ds(slots, 1)] = packed.reshape(n_tp, 1, cols // n_tp, DH)


def blocks(pieces, k_cache, v_cache, block_req, block_fill, n_tp):
    slots = k_cache.shape[0]
    cols = n_tp * pieces[0].shape[2]
    return pl.pallas_call(
        block_kernel,
        out_shape=jax.ShapeDtypeStruct((n_tp, slots + 1, cols // n_tp, DH), jnp.bfloat16),
        in_specs=[pl.BlockSpec(memory_space=pltpu.SMEM)] * 2
        + [pl.BlockSpec(memory_space=pl.ANY)] * (2 + len(pieces)),
        out_specs=pl.BlockSpec(memory_space=pltpu.VMEM),
        scratch_shapes=[
            pltpu.VMEM(k_cache.shape, k_cache.dtype),
            pltpu.VMEM(v_cache.shape, v_cache.dtype),
            pltpu.VMEM((slots,) + pieces[0].shape[:1] + pieces[0].shape[2:], pieces[0].dtype),
            pltpu.VMEM((DH, cols), jnp.float32),
            pltpu.SemaphoreType.DMA((3, slots)),
        ],
        compiler_params=pltpu.CompilerParams(vmem_limit_bytes=56 * 1024 * 1024),
        cost_estimate=pl.CostEstimate(
            flops=4 * slots * BLK * DH * 128, bytes_accessed=9 * 1024 * 1024, transcendentals=slots * BLK * 128
        ),
        name="blocks",
    )(block_req, block_fill, k_cache, v_cache, *pieces)


def combine(got, requests):
    n_src = got.shape[0]
    slots = got.shape[1] - 1
    n_cols = got.shape[2]
    every = n_src * (slots + 1)
    out = got.reshape(every, n_cols, DH)
    stats = got[:, slots, :, : 7 * slots].astype(jnp.float32)
    stats = stats.reshape(n_src, n_cols, 7, slots).transpose(2, 1, 0, 3)
    stats = jnp.pad(stats, ((0, 0), (0, 0), (0, 0), (0, 1)), constant_values=-1.0)
    stats = stats.reshape(7, n_cols, every)
    peak = stats[0] + stats[1] + stats[2]
    total = stats[3] + stats[4] + stats[5]
    owner = stats[6, 0].astype(jnp.int32)
    hot = owner[None, :] == jnp.arange(requests, dtype=jnp.int32)[:, None]
    masked = jnp.where(hot[None], peak[:, None, :], far_below)
    top = jnp.max(masked, axis=-1, keepdims=True)
    weight = jnp.where(hot[None], jnp.exp(masked - top), 0.0)
    den = jnp.sum(weight * total[:, None], axis=-1, keepdims=True)
    w_hi = lax.reduce_precision(weight, 8, 7)
    w_lo = (weight - w_hi).astype(jnp.bfloat16)
    w_hi = w_hi.astype(jnp.bfloat16)
    num = jnp.einsum("crj,jcd->crd", w_hi, out, preferred_element_type=jnp.float32) + jnp.einsum(
        "crj,jcd->crd", w_lo, out, preferred_element_type=jnp.float32
    )
    some = den > 0.0
    safe = jnp.where(some, den, 1.0)
    return num / safe, jnp.where(some, top + jnp.log(safe), far_below)


def fresh_kernel(kv, q_ref, keys_ref, values_ref, out_ref):
    n_steps, own_rows, width = q_ref.shape
    n_heads = width // DH
    lane = lax.broadcasted_iota(jnp.int32, (own_rows, DH), 1)
    levels = jnp.zeros((own_rows, DH), jnp.float32)
    for s in range(n_steps):
        for h in range(n_heads):
            c = s * n_heads + h
            query = q_ref[s, :, h * DH : (h + 1) * DH].astype(jnp.float32)
            fresh = [
                jnp.sum(query * keys_ref[j].astype(jnp.float32), axis=1, keepdims=True) * SCALE
                for j in range(s + 1)
            ]
            top = fresh[0]
            for x in fresh[1:]:
                top = jnp.maximum(top, x)
            num = jnp.zeros((own_rows, DH), jnp.float32)
            den = jnp.zeros((own_rows, 1), jnp.float32)
            for j in range(s + 1):
                weight = jnp.exp(fresh[j] - top)
                num = num + weight * values_ref[j].astype(jnp.float32)
                den = den + weight
            out_ref[c] = num / den
            levels = jnp.where(lane == c, top + jnp.log(den), levels)
    out_ref[n_steps * n_heads] = levels


def fresh_part(kv, queries, new_keys, new_values):
    n_steps, own_rows, width = queries.shape
    shape = (n_steps * (width // DH) + 1, own_rows, DH)
    own_kv = pl.BlockSpec((n_steps, own_rows, DH), lambda i, kv: (0, 0, kv[0]))
    return pl.pallas_call(
        fresh_kernel,
        out_shape=jax.ShapeDtypeStruct(shape, jnp.float32),
        grid_spec=pltpu.PrefetchScalarGridSpec(
            num_scalar_prefetch=1,
            grid=(1,),
            in_specs=[pl.BlockSpec(queries.shape, lambda i, kv: (0, 0, 0)), own_kv, own_kv],
            out_specs=pl.BlockSpec(shape, lambda i, kv: (0, 0, 0)),
        ),
        cost_estimate=pl.CostEstimate(flops=1 << 17, bytes_accessed=1 << 16, transcendentals=1 << 8),
        name="fresh",
    )(kv, queries, new_keys, new_values)


def finish_kernel(got, fresh, out_ref):
    n_steps, own_rows, width = out_ref.shape
    n_heads = width // DH
    last = n_steps * n_heads
    parts = [got.at[i] for i in range(got.shape[0])] + [fresh]
    levels = [part[last] for part in parts]
    top = levels[0]
    for x in levels[1:]:
        top = jnp.maximum(top, x)
    weights = [jnp.exp(x - top) for x in levels]
    den = weights[0]
    for x in weights[1:]:
        den = den + x
    inverse = 1.0 / den
    weights = [x * inverse for x in weights]
    for s in range(n_steps):
        for h in range(n_heads):
            c = s * n_heads + h
            num = jnp.zeros((own_rows, DH), jnp.float32)
            for weight, part in zip(weights, parts):
                num = num + weight[:, c : c + 1] * part[c]
            out_ref[s, :, h * DH : (h + 1) * DH] = num.astype(out_ref.dtype)


def finish(got, fresh, n_steps):
    own_rows = got.shape[2]
    width = (got.shape[1] - 1) // n_steps * DH
    return pl.pallas_call(
        finish_kernel,
        out_shape=jax.ShapeDtypeStruct((n_steps, own_rows, width), jnp.bfloat16),
        in_specs=[pl.BlockSpec(memory_space=pltpu.VMEM)] * 2,
        out_specs=pl.BlockSpec(memory_space=pltpu.VMEM),
        name="finish",
    )(got, fresh)


def body(queries, new_keys, new_values, k_cache, v_cache, block_req, block_fill):
    n_steps, own_rows, width = queries.shape
    own_heads = width // DH
    n_y, n_core = lax.axis_size("y"), lax.axis_size("core")
    n_z, n_x = lax.axis_size("z"), lax.axis_size("x")
    n_inst = n_y * n_core

    def from_other(value, axis, m):
        return lax.ppermute(value, axis, [(j, j ^ m) for j in range(lax.axis_size(axis))])

    rows = queries.reshape(n_steps, own_rows, own_heads, DH).transpose(1, 0, 2, 3)
    rows = rows.reshape(own_rows, n_steps * own_heads, DH)
    own = lax.all_to_all(
        jnp.broadcast_to(rows[None], (n_z * n_x,) + rows.shape), ("z", "x"), 0, 0, tiled=True
    )
    pieces = [own] + [from_other(own, "y", m) for m in range(1, n_y)]
    pieces = pieces + [from_other(p, "core", 1) for p in pieces]
    sent = blocks(pieces, k_cache, v_cache, block_req, block_fill, n_z * n_x)
    kv = lax.axis_index("z").astype(jnp.int32).reshape(1)
    sent, kv = lax.optimization_barrier((sent, kv))
    got = lax.all_to_all(sent, ("z", "x"), split_axis=0, concat_axis=0, tiled=True)
    got, fresh = lax.optimization_barrier((got, fresh_part(kv, queries, new_keys, new_values)))
    part, level = combine(got, n_inst * own_rows)
    level = level[..., 0].reshape(4, n_inst, own_rows).transpose(1, 2, 0)
    level = jnp.pad(level, ((0, 0), (0, 0), (0, DH - 4)))[:, None]
    part = part.reshape(4, n_inst, own_rows, DH).transpose(1, 0, 2, 3)
    both = lax.all_to_all(
        jnp.concatenate([part, level], axis=1), ("y", "core"), 0, 0, tiled=True
    )
    return finish(both, fresh, n_steps)


def solution(mesh):
    n_inst, n_tp = mesh.devices.shape
    split = Mesh(
        mesh.devices.reshape(n_inst // 2, 2, KVH, n_tp // KVH), ("y", "core", "z", "x")
    )
    inst, tp = ("y", "core"), ("z", "x")
    return jax.shard_map(
        body,
        mesh=split,
        in_specs=(
            P(None, inst, tp),
            P(None, inst, None),
            P(None, inst, None),
            P(inst + tp, None, None),
            P(inst + tp, None, None),
            P(inst + tp),
            P(inst + tp),
        ),
        out_specs=P(None, inst, tp),
        check_vma=False,
    )
```

```python
import jax
import jax.numpy as jnp
from jax import lax
from jax.experimental import pallas as pl
from jax.experimental.pallas import tpu as pltpu
from jax.sharding import Mesh, PartitionSpec as P

H = 64
KVH = 8
DH = 128
BLK = 128
SCALE = DH ** (-0.5)

far_below = -1e30


def split_three(x):
    hi = x.astype(jnp.bfloat16)
    rest = x - hi.astype(jnp.float32)
    mid = rest.astype(jnp.bfloat16)
    lo = (rest - mid.astype(jnp.float32)).astype(jnp.bfloat16)
    return hi, mid, lo


def block_kernel(owner, fill, k_hbm, v_hbm, *refs):
    pieces = refs[:-6]
    out_ref, k_all, v_all, picked, stats, sem = refs[-6:]
    slots, n_tp, depth, _ = picked.shape
    cols = n_tp * depth
    n_kv = KVH
    per, n_x = cols // n_kv, n_tp // n_kv
    together = 4
    rows = pieces[0].shape[2]
    n_core = 2
    here_y, here_core = lax.axis_index("y"), lax.axis_index("core")

    def fetch(b):
        home = owner[b] // rows
        row = lax.rem(owner[b], rows)
        core = lax.rem(home, n_core)
        away = home // n_core ^ here_y
        odd = lax.rem(away, 2)
        half = (away // 2) ^ (odd * core)
        which = odd + (core ^ here_core) * 2
        for p, piece in enumerate(pieces):

            @pl.when(which == p)
            def _(piece=piece):
                pltpu.make_async_copy(piece.at[:, half, row], picked.at[b], sem.at[2, b]).start()

    def copies(b):
        return (
            pltpu.make_async_copy(k_hbm.at[b], k_all.at[b], sem.at[0, b]),
            pltpu.make_async_copy(v_hbm.at[b], v_all.at[b], sem.at[1, b]),
        )

    def start(b, _):
        fetch(b)
        for c in copies(b):
            c.start()
        return 0

    lax.fori_loop(0, 2 * together, start, 0)
    stats[...] = jnp.zeros_like(stats)
    slot_at = lax.broadcasted_iota(jnp.int32, (BLK, cols), 0)
    nothing = jnp.zeros((per, DH), jnp.bfloat16)

    def score(b):
        spread = []
        for g in range(n_kv):
            mine = picked[b, g * n_x : (g + 1) * n_x].reshape(per, DH)
            spread.append(
                jnp.concatenate([nothing] * g + [mine] + [nothing] * (n_kv - 1 - g), axis=1)
            )
        scores = lax.dot_general(
            k_all[b],
            jnp.concatenate(spread, axis=0),
            (((1,), (1,)), ((), ())),
            preferred_element_type=jnp.float32,
        )
        return jnp.where(slot_at < fill[b], scores * SCALE, far_below)

    def soften(b, scores):
        peak = jnp.max(scores, axis=0, keepdims=True)
        chances = jnp.exp(scores - peak)
        total = jnp.sum(chances, axis=0, keepdims=True)
        for p, piece in enumerate(split_three(peak) + split_three(total)):
            stats[pl.ds(p * slots + b, 1)] = piece.astype(jnp.float32)
        stats[pl.ds(6 * slots + b, 1)] = jnp.broadcast_to(owner[b].astype(jnp.float32), (1, cols))
        return chances.astype(jnp.bfloat16).T

    def mix(b, rounded):
        mixed = []
        for g in range(0, n_kv, 2):
            two = jnp.dot(
                rounded[g * per : (g + 2) * per],
                v_all[b, :, g * DH : (g + 2) * DH],
                preferred_element_type=jnp.float32,
            ).astype(jnp.bfloat16)
            mixed = mixed + [two[:per, :DH], two[per:, DH:]]
        mixed = jnp.concatenate(mixed, axis=0)
        out_ref[:, pl.ds(b, 1)] = mixed.reshape(n_tp, 1, cols // n_tp, DH)

    def some_blocks(i, _):
        first = i * together

        @pl.when(first + 2 * together < slots)
        def _():
            lax.fori_loop(first + 2 * together, first + 3 * together, start, 0)

        for j in range(together):
            for c in copies(first + j):
                c.wait()
            pltpu.make_async_copy(pieces[0].at[:, 0, 0], picked.at[first + j], sem.at[2, first + j]).wait()
        scores = [score(first + j) for j in range(together)]
        rounded = [soften(first + j, scores[j]) for j in range(together)]
        for j in range(together):
            mix(first + j, rounded[j])
        return 0

    lax.fori_loop(0, slots // together, some_blocks, 0)
    packed = stats[...].T.astype(jnp.bfloat16)
    out_ref[:, pl.ds(slots, 1)] = packed.reshape(n_tp, 1, cols // n_tp, DH)


def blocks(pieces, k_cache, v_cache, block_req, block_fill, n_tp):
    slots = k_cache.shape[0]
    cols = n_tp * pieces[0].shape[3]
    return pl.pallas_call(
        block_kernel,
        out_shape=jax.ShapeDtypeStruct((n_tp, slots + 1, cols // n_tp, DH), jnp.bfloat16),
        in_specs=[pl.BlockSpec(memory_space=pltpu.SMEM)] * 2
        + [pl.BlockSpec(memory_space=pl.ANY)] * (2 + len(pieces)),
        out_specs=pl.BlockSpec(memory_space=pltpu.VMEM),
        scratch_shapes=[
            pltpu.VMEM(k_cache.shape, k_cache.dtype),
            pltpu.VMEM(v_cache.shape, v_cache.dtype),
            pltpu.VMEM((slots,) + pieces[0].shape[:1] + pieces[0].shape[3:], pieces[0].dtype),
            pltpu.VMEM((DH, cols), jnp.float32),
            pltpu.SemaphoreType.DMA((3, slots)),
        ],
        compiler_params=pltpu.CompilerParams(vmem_limit_bytes=56 * 1024 * 1024),
        cost_estimate=pl.CostEstimate(
            flops=4 * slots * BLK * DH * 128, bytes_accessed=9 * 1024 * 1024, transcendentals=slots * BLK * 128
        ),
        name="blocks",
    )(block_req, block_fill, k_cache, v_cache, *pieces)


def combine(got, requests):
    n_src = got.shape[0]
    slots = got.shape[1] - 1
    n_cols = got.shape[2]
    every = n_src * (slots + 1)
    out = got.reshape(every, n_cols, DH)
    stats = got[:, slots, :, : 7 * slots].astype(jnp.float32)
    stats = stats.reshape(n_src, n_cols, 7, slots).transpose(2, 1, 0, 3)
    stats = jnp.pad(stats, ((0, 0), (0, 0), (0, 0), (0, 1)), constant_values=-1.0)
    stats = stats.reshape(7, n_cols, every)
    peak = stats[0] + stats[1] + stats[2]
    total = stats[3] + stats[4] + stats[5]
    owner = stats[6, 0].astype(jnp.int32)
    hot = owner[None, :] == jnp.arange(requests, dtype=jnp.int32)[:, None]
    masked = jnp.where(hot[None], peak[:, None, :], far_below)
    top = jnp.max(masked, axis=-1, keepdims=True)
    weight = jnp.where(hot[None], jnp.exp(masked - top), 0.0)
    den = jnp.sum(weight * total[:, None], axis=-1, keepdims=True)
    w_hi = lax.reduce_precision(weight, 8, 7)
    w_lo = (weight - w_hi).astype(jnp.bfloat16)
    w_hi = w_hi.astype(jnp.bfloat16)
    num = jnp.einsum("crj,jcd->crd", w_hi, out, preferred_element_type=jnp.float32) + jnp.einsum(
        "crj,jcd->crd", w_lo, out, preferred_element_type=jnp.float32
    )
    some = den > 0.0
    safe = jnp.where(some, den, 1.0)
    return num / safe, jnp.where(some, top + jnp.log(safe), far_below)


def fresh_kernel(kv, q_ref, keys_ref, values_ref, out_ref):
    n_steps, own_rows, width = q_ref.shape
    n_heads = width // DH
    lane = lax.broadcasted_iota(jnp.int32, (own_rows, DH), 1)
    levels = jnp.zeros((own_rows, DH), jnp.float32)
    for s in range(n_steps):
        for h in range(n_heads):
            c = s * n_heads + h
            query = q_ref[s, :, h * DH : (h + 1) * DH].astype(jnp.float32)
            fresh = [
                jnp.sum(query * keys_ref[j].astype(jnp.float32), axis=1, keepdims=True) * SCALE
                for j in range(s + 1)
            ]
            top = fresh[0]
            for x in fresh[1:]:
                top = jnp.maximum(top, x)
            num = jnp.zeros((own_rows, DH), jnp.float32)
            den = jnp.zeros((own_rows, 1), jnp.float32)
            for j in range(s + 1):
                weight = jnp.exp(fresh[j] - top)
                num = num + weight * values_ref[j].astype(jnp.float32)
                den = den + weight
            out_ref[c] = num / den
            levels = jnp.where(lane == c, top + jnp.log(den), levels)
    out_ref[n_steps * n_heads] = levels


def fresh_part(kv, queries, new_keys, new_values):
    n_steps, own_rows, width = queries.shape
    shape = (n_steps * (width // DH) + 1, own_rows, DH)
    own_kv = pl.BlockSpec((n_steps, own_rows, DH), lambda i, kv: (0, 0, kv[0]))
    return pl.pallas_call(
        fresh_kernel,
        out_shape=jax.ShapeDtypeStruct(shape, jnp.float32),
        grid_spec=pltpu.PrefetchScalarGridSpec(
            num_scalar_prefetch=1,
            grid=(1,),
            in_specs=[pl.BlockSpec(queries.shape, lambda i, kv: (0, 0, 0)), own_kv, own_kv],
            out_specs=pl.BlockSpec(shape, lambda i, kv: (0, 0, 0)),
        ),
        cost_estimate=pl.CostEstimate(flops=1 << 17, bytes_accessed=1 << 16, transcendentals=1 << 8),
        name="fresh",
    )(kv, queries, new_keys, new_values)


def finish_kernel(got, fresh, out_ref):
    n_steps, own_rows, width = out_ref.shape
    n_heads = width // DH
    last = n_steps * n_heads
    parts = [got.at[i] for i in range(got.shape[0])] + [fresh]
    levels = [part[last] for part in parts]
    top = levels[0]
    for x in levels[1:]:
        top = jnp.maximum(top, x)
    weights = [jnp.exp(x - top) for x in levels]
    den = weights[0]
    for x in weights[1:]:
        den = den + x
    inverse = 1.0 / den
    weights = [x * inverse for x in weights]
    for s in range(n_steps):
        for h in range(n_heads):
            c = s * n_heads + h
            num = jnp.zeros((own_rows, DH), jnp.float32)
            for weight, part in zip(weights, parts):
                num = num + weight[:, c : c + 1] * part[c]
            out_ref[s, :, h * DH : (h + 1) * DH] = num.astype(out_ref.dtype)


def finish(got, fresh, n_steps):
    own_rows = got.shape[2]
    width = (got.shape[1] - 1) // n_steps * DH
    return pl.pallas_call(
        finish_kernel,
        out_shape=jax.ShapeDtypeStruct((n_steps, own_rows, width), jnp.bfloat16),
        in_specs=[pl.BlockSpec(memory_space=pltpu.VMEM)] * 2,
        out_specs=pl.BlockSpec(memory_space=pltpu.VMEM),
        name="finish",
    )(got, fresh)


def body(queries, new_keys, new_values, k_cache, v_cache, block_req, block_fill):
    n_steps, own_rows, width = queries.shape
    own_heads = width // DH
    n_y, n_core = lax.axis_size("y"), lax.axis_size("core")
    n_z, n_x = lax.axis_size("z"), lax.axis_size("x")
    n_inst = n_y * n_core

    def from_other(value, axis, m):
        return lax.ppermute(value, axis, [(j, j ^ m) for j in range(lax.axis_size(axis))])

    rows = queries.reshape(n_steps, own_rows, own_heads, DH).transpose(1, 0, 2, 3)
    rows = rows.reshape(own_rows, n_steps * own_heads, DH)
    rows = jnp.stack([rows, from_other(rows, "y", 2)])
    own = lax.all_to_all(
        jnp.broadcast_to(rows[None], (n_z * n_x,) + rows.shape), ("z", "x"), 0, 0, tiled=True
    )
    partner = [
        (y * n_core + c, (y ^ (1, 3)[c]) * n_core + c) for y in range(n_y) for c in range(n_core)
    ]
    pieces = [own, lax.ppermute(own, ("y", "core"), partner)]
    pieces = pieces + [from_other(p, "core", 1) for p in pieces]
    sent = blocks(pieces, k_cache, v_cache, block_req, block_fill, n_z * n_x)
    kv = lax.axis_index("z").astype(jnp.int32).reshape(1)
    sent, kv = lax.optimization_barrier((sent, kv))
    got = lax.all_to_all(sent, ("z", "x"), split_axis=0, concat_axis=0, tiled=True)
    got, fresh = lax.optimization_barrier((got, fresh_part(kv, queries, new_keys, new_values)))
    part, level = combine(got, n_inst * own_rows)
    level = level[..., 0].reshape(4, n_inst, own_rows).transpose(1, 2, 0)
    level = jnp.pad(level, ((0, 0), (0, 0), (0, DH - 4)))[:, None]
    part = part.reshape(4, n_inst, own_rows, DH).transpose(1, 0, 2, 3)
    both = lax.all_to_all(
        jnp.concatenate([part, level], axis=1), ("y", "core"), 0, 0, tiled=True
    )
    return finish(both, fresh, n_steps)


def solution(mesh):
    n_inst, n_tp = mesh.devices.shape
    split = Mesh(
        mesh.devices.reshape(n_inst // 2, 2, KVH, n_tp // KVH), ("y", "core", "z", "x")
    )
    inst, tp = ("y", "core"), ("z", "x")
    return jax.shard_map(
        body,
        mesh=split,
        in_specs=(
            P(None, inst, tp),
            P(None, inst, None),
            P(None, inst, None),
            P(inst + tp, None, None),
            P(inst + tp, None, None),
            P(inst + tp),
            P(inst + tp),
        ),
        out_specs=P(None, inst, tp),
        check_vma=False,
    )
```

```python
import math
import jax
import jax.numpy as jnp
from jax import lax
from jax.experimental import pallas as pl
from jax.experimental.pallas import tpu as pltpu
from jax.sharding import Mesh, PartitionSpec as P

H = 64
KVH = 8
DH = 128
BLK = 128
SCALE = DH ** (-0.5)

far_below = -1e30


def split_three(x):
    hi = x.astype(jnp.bfloat16)
    rest = x - hi.astype(jnp.float32)
    mid = rest.astype(jnp.bfloat16)
    lo = (rest - mid.astype(jnp.float32)).astype(jnp.bfloat16)
    return hi, mid, lo


def block_kernel(owner, fill, k_hbm, v_hbm, *refs):
    pieces = refs[:-6]
    out_ref, k_all, v_all, picked, stats, sem = refs[-6:]
    slots, n_tp, depth, _ = picked.shape
    cols = n_tp * depth
    n_kv = KVH
    per, n_x = cols // n_kv, n_tp // n_kv
    together = 4
    rows = pieces[0].shape[1]
    n_core = 2
    n_y = len(pieces) // n_core
    here_y, here_core = lax.axis_index("y"), lax.axis_index("core")

    def fetch(b):
        home = owner[b] // rows
        row = lax.rem(owner[b], rows)
        away = home // n_core ^ here_y
        which = lax.rem(n_y - away, n_y) + (lax.rem(home, n_core) ^ here_core) * n_y
        for p, piece in enumerate(pieces):

            @pl.when(which == p)
            def _(piece=piece):
                pltpu.make_async_copy(piece.at[:, row], picked.at[b], sem.at[2, b]).start()

    def copies(b):
        return (
            pltpu.make_async_copy(k_hbm.at[b], k_all.at[b], sem.at[0, b]),
            pltpu.make_async_copy(v_hbm.at[b], v_all.at[b], sem.at[1, b]),
        )

    def start(b, _):
        fetch(b)
        for c in copies(b):
            c.start()
        return 0

    lax.fori_loop(0, slots, start, 0)
    stats[...] = jnp.zeros_like(stats)
    slot_at = lax.broadcasted_iota(jnp.int32, (BLK, cols), 0)
    head = lax.broadcasted_iota(jnp.int32, (DH, cols), 1) // per

    def score(b):
        query = picked[b].reshape(cols, DH).T
        nothing = jnp.zeros_like(query)
        spread = [jnp.where(head == g, query, nothing) for g in range(n_kv)]
        scores = jnp.dot(
            k_all[b], jnp.concatenate(spread, axis=0), preferred_element_type=jnp.float32
        )
        return jnp.where(slot_at < fill[b], scores, far_below)

    def soften(b, scores):
        peak = jnp.max(scores, axis=0, keepdims=True)
        chances = jnp.exp2((scores - peak) * (SCALE * math.log2(math.e)))
        total = jnp.sum(chances, axis=0, keepdims=True)
        for p, piece in enumerate(split_three(peak * SCALE) + split_three(total)):
            stats[pl.ds(p * slots + b, 1)] = piece.astype(jnp.float32)
        stats[pl.ds(6 * slots + b, 1)] = jnp.broadcast_to(owner[b].astype(jnp.float32), (1, cols))
        return chances.astype(jnp.bfloat16).T

    def mix(b, rounded):
        mixed = []
        for g in range(0, n_kv, 2):
            two = jnp.dot(
                rounded[g * per : (g + 2) * per],
                v_all[b, :, g * DH : (g + 2) * DH],
                preferred_element_type=jnp.float32,
            ).astype(jnp.bfloat16)
            mixed = mixed + [two[:per, :DH], two[per:, DH:]]
        mixed = jnp.concatenate(mixed, axis=0)
        out_ref[:, pl.ds(b, 1)] = mixed.reshape(n_tp, 1, cols // n_tp, DH)

    def some_blocks(i, _):
        first = i * together
        for j in range(together):
            for c in copies(first + j):
                c.wait()
            pltpu.make_async_copy(pieces[0].at[:, 0], picked.at[first + j], sem.at[2, first + j]).wait()
        scores = [score(first + j) for j in range(together)]
        rounded = [soften(first + j, scores[j]) for j in range(together)]
        for j in range(together):
            mix(first + j, rounded[j])
        return 0

    lax.fori_loop(0, slots // together, some_blocks, 0)
    packed = stats[...].T.astype(jnp.bfloat16)
    out_ref[:, pl.ds(slots, 1)] = packed.reshape(n_tp, 1, cols // n_tp, DH)


def blocks(pieces, k_cache, v_cache, block_req, block_fill, n_tp):
    slots = k_cache.shape[0]
    cols = n_tp * pieces[0].shape[2]
    return pl.pallas_call(
        block_kernel,
        out_shape=jax.ShapeDtypeStruct((n_tp, slots + 1, cols // n_tp, DH), jnp.bfloat16),
        in_specs=[pl.BlockSpec(memory_space=pltpu.SMEM)] * 2
        + [pl.BlockSpec(memory_space=pl.ANY)] * (2 + len(pieces)),
        out_specs=pl.BlockSpec(memory_space=pltpu.VMEM),
        scratch_shapes=[
            pltpu.VMEM(k_cache.shape, k_cache.dtype),
            pltpu.VMEM(v_cache.shape, v_cache.dtype),
            pltpu.VMEM((slots,) + pieces[0].shape[:1] + pieces[0].shape[2:], pieces[0].dtype),
            pltpu.VMEM((DH, cols), jnp.float32),
            pltpu.SemaphoreType.DMA((3, slots)),
        ],
        compiler_params=pltpu.CompilerParams(vmem_limit_bytes=56 * 1024 * 1024),
        cost_estimate=pl.CostEstimate(
            flops=4 * slots * BLK * DH * 128, bytes_accessed=9 * 1024 * 1024, transcendentals=slots * BLK * 128
        ),
        name="blocks",
    )(block_req, block_fill, k_cache, v_cache, *pieces)


def combine(got, requests):
    n_src = got.shape[0]
    slots = got.shape[1] - 1
    n_cols = got.shape[2]
    every = n_src * (slots + 1)
    out = got.reshape(every, n_cols, DH)
    stats = got[:, slots]

    def three(first):
        pieces = [stats[:, :, (first + p) * slots : (first + p + 1) * slots] for p in range(3)]
        hi, mid, lo = [piece.astype(jnp.float32) for piece in pieces]
        value = jnp.pad(hi + mid + lo, ((0, 0), (0, 0), (0, 1)))
        return value.transpose(1, 0, 2).reshape(n_cols, every)

    peak, total = three(0), three(3)
    owner = stats[:, 0, 6 * slots : 7 * slots].astype(jnp.int32)
    owner = jnp.pad(owner, ((0, 0), (0, 1)), constant_values=-1).reshape(every)
    hot = owner[None, :] == jnp.arange(requests, dtype=jnp.int32)[:, None]
    masked = jnp.where(hot[None], peak[:, None, :], far_below)
    top = jnp.max(masked, axis=-1, keepdims=True)
    weight = jnp.where(hot[None], jnp.exp(masked - top), 0.0)
    den = jnp.sum(weight * total[:, None], axis=-1, keepdims=True)
    w_hi = lax.reduce_precision(weight, 8, 7)
    w_lo = (weight - w_hi).astype(jnp.bfloat16)
    w_hi = w_hi.astype(jnp.bfloat16)
    num = jnp.einsum("crj,jcd->crd", w_hi, out, preferred_element_type=jnp.float32) + jnp.einsum(
        "crj,jcd->crd", w_lo, out, preferred_element_type=jnp.float32
    )
    some = den > 0.0
    safe = jnp.where(some, den, 1.0)
    return num / safe, jnp.where(some, top + jnp.log(safe), far_below)


def fresh_kernel(kv, q_ref, keys_ref, values_ref, out_ref):
    n_steps, own_rows, width = q_ref.shape
    n_heads = width // DH
    lane = lax.broadcasted_iota(jnp.int32, (own_rows, DH), 1)
    levels = jnp.zeros((own_rows, DH), jnp.float32)
    for s in range(n_steps):
        for h in range(n_heads):
            c = s * n_heads + h
            query = q_ref[s, :, h * DH : (h + 1) * DH].astype(jnp.float32)
            fresh = [
                jnp.sum(query * keys_ref[j].astype(jnp.float32), axis=1, keepdims=True) * SCALE
                for j in range(s + 1)
            ]
            top = fresh[0]
            for x in fresh[1:]:
                top = jnp.maximum(top, x)
            num = jnp.zeros((own_rows, DH), jnp.float32)
            den = jnp.zeros((own_rows, 1), jnp.float32)
            for j in range(s + 1):
                weight = jnp.exp(fresh[j] - top)
                num = num + weight * values_ref[j].astype(jnp.float32)
                den = den + weight
            out_ref[c] = num / den
            levels = jnp.where(lane == c, top + jnp.log(den), levels)
    out_ref[n_steps * n_heads] = levels


def fresh_part(kv, queries, new_keys, new_values):
    n_steps, own_rows, width = queries.shape
    shape = (n_steps * (width // DH) + 1, own_rows, DH)
    own_kv = pl.BlockSpec((n_steps, own_rows, DH), lambda i, kv: (0, 0, kv[0]))
    return pl.pallas_call(
        fresh_kernel,
        out_shape=jax.ShapeDtypeStruct(shape, jnp.float32),
        grid_spec=pltpu.PrefetchScalarGridSpec(
            num_scalar_prefetch=1,
            grid=(1,),
            in_specs=[pl.BlockSpec(queries.shape, lambda i, kv: (0, 0, 0)), own_kv, own_kv],
            out_specs=pl.BlockSpec(shape, lambda i, kv: (0, 0, 0)),
        ),
        cost_estimate=pl.CostEstimate(flops=1 << 17, bytes_accessed=1 << 16, transcendentals=1 << 8),
        name="fresh",
    )(kv, queries, new_keys, new_values)


def finish_kernel(got, fresh, out_ref):
    n_steps, own_rows, width = out_ref.shape
    n_heads = width // DH
    last = n_steps * n_heads
    parts = [got.at[i] for i in range(got.shape[0])] + [fresh]
    levels = [part[last] for part in parts]
    top = levels[0]
    for x in levels[1:]:
        top = jnp.maximum(top, x)
    weights = [jnp.exp(x - top) for x in levels]
    den = weights[0]
    for x in weights[1:]:
        den = den + x
    inverse = 1.0 / den
    weights = [x * inverse for x in weights]
    for s in range(n_steps):
        for h in range(n_heads):
            c = s * n_heads + h
            num = jnp.zeros((own_rows, DH), jnp.float32)
            for weight, part in zip(weights, parts):
                num = num + weight[:, c : c + 1] * part[c]
            out_ref[s, :, h * DH : (h + 1) * DH] = num.astype(out_ref.dtype)


def finish(got, fresh, n_steps):
    own_rows = got.shape[2]
    width = (got.shape[1] - 1) // n_steps * DH
    return pl.pallas_call(
        finish_kernel,
        out_shape=jax.ShapeDtypeStruct((n_steps, own_rows, width), jnp.bfloat16),
        in_specs=[pl.BlockSpec(memory_space=pltpu.VMEM)] * 2,
        out_specs=pl.BlockSpec(memory_space=pltpu.VMEM),
        name="finish",
    )(got, fresh)


def body(queries, new_keys, new_values, k_cache, v_cache, block_req, block_fill):
    n_steps, own_rows, width = queries.shape
    own_heads = width // DH
    n_y, n_core = lax.axis_size("y"), lax.axis_size("core")
    n_z, n_x = lax.axis_size("z"), lax.axis_size("x")
    n_inst = n_y * n_core

    def from_other(value, axis, m):
        return lax.ppermute(value, axis, [(j, j ^ m) for j in range(lax.axis_size(axis))])

    rows = queries.reshape(n_steps, own_rows, own_heads, DH).transpose(1, 0, 2, 3)
    rows = rows.reshape(own_rows, n_steps * own_heads, DH)
    own = lax.all_to_all(
        jnp.broadcast_to(rows[None], (n_z * n_x,) + rows.shape), ("z", "x"), 0, 0, tiled=True
    )
    pieces = [own] + [from_other(own, "y", m) for m in range(n_y - 1, 0, -1)]
    pieces = pieces + [from_other(p, "core", 1) for p in pieces]
    sent = blocks(pieces, k_cache, v_cache, block_req, block_fill, n_z * n_x)
    kv = lax.axis_index("z").astype(jnp.int32).reshape(1)
    sent, kv = lax.optimization_barrier((sent, kv))
    got = lax.all_to_all(sent, ("z", "x"), split_axis=0, concat_axis=0, tiled=True)
    got, fresh = lax.optimization_barrier((got, fresh_part(kv, queries, new_keys, new_values)))
    part, level = combine(got, n_inst * own_rows)
    level = level[..., 0].reshape(4, n_inst, own_rows).transpose(1, 2, 0)
    level = jnp.pad(level, ((0, 0), (0, 0), (0, DH - 4)))[:, None]
    part = part.reshape(4, n_inst, own_rows, DH).transpose(1, 0, 2, 3)
    both = lax.all_to_all(
        jnp.concatenate([part, level], axis=1), ("y", "core"), 0, 0, tiled=True
    )
    return finish(both, fresh, n_steps)


def solution(mesh):
    n_inst, n_tp = mesh.devices.shape
    split = Mesh(
        mesh.devices.reshape(n_inst // 2, 2, KVH, n_tp // KVH), ("y", "core", "z", "x")
    )
    inst, tp = ("y", "core"), ("z", "x")
    return jax.shard_map(
        body,
        mesh=split,
        in_specs=(
            P(None, inst, tp),
            P(None, inst, None),
            P(None, inst, None),
            P(inst + tp, None, None),
            P(inst + tp, None, None),
            P(inst + tp),
            P(inst + tp),
        ),
        out_specs=P(None, inst, tp),
        check_vma=False,
    )
```

```python
import math
import jax
import jax.numpy as jnp
from jax import lax
from jax.experimental import pallas as pl
from jax.experimental.pallas import tpu as pltpu
from jax.sharding import Mesh, PartitionSpec as P

H = 64
KVH = 8
DH = 128
BLK = 128
SCALE = DH ** (-0.5)

far_below = -1e30


def split_three(x):
    hi = x.astype(jnp.bfloat16)
    rest = x - hi.astype(jnp.float32)
    mid = rest.astype(jnp.bfloat16)
    lo = (rest - mid.astype(jnp.float32)).astype(jnp.bfloat16)
    return hi, mid, lo


def block_kernel(owner, fill, k_hbm, v_hbm, *refs):
    pieces = refs[:-6]
    out_ref, k_all, v_all, picked, stats, sem = refs[-6:]
    slots, n_tp, depth, _ = picked.shape
    cols = n_tp * depth
    n_kv = KVH
    per, n_x = cols // n_kv, n_tp // n_kv
    together = 4
    rows = pieces[0].shape[1]
    n_core = 2
    n_y = len(pieces) // n_core
    here_y, here_core = lax.axis_index("y"), lax.axis_index("core")

    def fetch(b):
        home = owner[b] // rows
        row = lax.rem(owner[b], rows)
        away = home // n_core ^ here_y
        which = lax.rem(n_y - away, n_y) + (lax.rem(home, n_core) ^ here_core) * n_y
        for p, piece in enumerate(pieces):

            @pl.when(which == p)
            def _(piece=piece):
                pltpu.make_async_copy(piece.at[:, row], picked.at[b], sem.at[2, b]).start()

    def keys_of(b):
        return pltpu.make_async_copy(k_hbm.at[b], k_all.at[b], sem.at[0, b])

    def values_of(b):
        return pltpu.make_async_copy(v_hbm.at[b], v_all.at[b], sem.at[1, b])

    def start(b, _):
        keys_of(b).start()
        fetch(b)
        return 0

    def start_values(b, _):
        values_of(b).start()
        return 0

    groups = slots // together
    for g in range(groups):
        lax.fori_loop(g * together, (g + 1) * together, start, 0)
        if g:
            lax.fori_loop((g - 1) * together, g * together, start_values, 0)
    lax.fori_loop((groups - 1) * together, slots, start_values, 0)
    stats[...] = jnp.zeros_like(stats)
    slot_at = lax.broadcasted_iota(jnp.int32, (BLK, cols), 0)
    head = lax.broadcasted_iota(jnp.int32, (DH, cols), 1) // per

    def score(b):
        query = picked[b].reshape(cols, DH).T
        nothing = jnp.zeros_like(query)
        spread = [jnp.where(head == g, query, nothing) for g in range(n_kv)]
        scores = jnp.dot(
            k_all[b], jnp.concatenate(spread, axis=0), preferred_element_type=jnp.float32
        )
        return jnp.where(slot_at < fill[b], scores, far_below)

    def soften(b, scores):
        peak = jnp.max(scores, axis=0, keepdims=True)
        chances = jnp.exp2((scores - peak) * (SCALE * math.log2(math.e)))
        total = jnp.sum(chances, axis=0, keepdims=True)
        for p, piece in enumerate(split_three(peak * SCALE) + split_three(total)):
            stats[pl.ds(p * slots + b, 1)] = piece.astype(jnp.float32)
        stats[pl.ds(6 * slots + b, 1)] = jnp.broadcast_to(owner[b].astype(jnp.float32), (1, cols))
        return chances.astype(jnp.bfloat16).T

    def mix(b, rounded):
        mixed = []
        for g in range(0, n_kv, 2):
            two = jnp.dot(
                rounded[g * per : (g + 2) * per],
                v_all[b, :, g * DH : (g + 2) * DH],
                preferred_element_type=jnp.float32,
            ).astype(jnp.bfloat16)
            mixed = mixed + [two[:per, :DH], two[per:, DH:]]
        mixed = jnp.concatenate(mixed, axis=0)
        out_ref[:, pl.ds(b, 1)] = mixed.reshape(n_tp, 1, cols // n_tp, DH)

    def weigh(first):
        for j in range(together):
            keys_of(first + j).wait()
            pltpu.make_async_copy(pieces[0].at[:, 0], picked.at[first + j], sem.at[2, first + j]).wait()
        scores = [score(first + j) for j in range(together)]
        return tuple(soften(first + j, scores[j]) for j in range(together))

    def await_values(first):
        for j in range(together):
            values_of(first + j).wait()

    def step(i, rounded):
        first = i * together
        await_values(first)
        later = weigh(first + together)
        for j in range(together):
            mix(first + j, rounded[j])
        return later

    rounded = lax.fori_loop(0, groups - 1, step, weigh(0))
    await_values(slots - together)
    for j in range(together):
        mix(slots - together + j, rounded[j])
    packed = stats[...].T.astype(jnp.bfloat16)
    out_ref[:, pl.ds(slots, 1)] = packed.reshape(n_tp, 1, cols // n_tp, DH)


def blocks(pieces, k_cache, v_cache, block_req, block_fill, n_tp):
    slots = k_cache.shape[0]
    cols = n_tp * pieces[0].shape[2]
    return pl.pallas_call(
        block_kernel,
        out_shape=jax.ShapeDtypeStruct((n_tp, slots + 1, cols // n_tp, DH), jnp.bfloat16),
        in_specs=[pl.BlockSpec(memory_space=pltpu.SMEM)] * 2
        + [pl.BlockSpec(memory_space=pl.ANY)] * (2 + len(pieces)),
        out_specs=pl.BlockSpec(memory_space=pltpu.VMEM),
        scratch_shapes=[
            pltpu.VMEM(k_cache.shape, k_cache.dtype),
            pltpu.VMEM(v_cache.shape, v_cache.dtype),
            pltpu.VMEM((slots,) + pieces[0].shape[:1] + pieces[0].shape[2:], pieces[0].dtype),
            pltpu.VMEM((DH, cols), jnp.float32),
            pltpu.SemaphoreType.DMA((3, slots)),
        ],
        compiler_params=pltpu.CompilerParams(vmem_limit_bytes=56 * 1024 * 1024),
        cost_estimate=pl.CostEstimate(
            flops=4 * slots * BLK * DH * 128, bytes_accessed=9 * 1024 * 1024, transcendentals=slots * BLK * 128
        ),
        name="blocks",
    )(block_req, block_fill, k_cache, v_cache, *pieces)


def combine(got, requests):
    n_src = got.shape[0]
    slots = got.shape[1] - 1
    n_cols = got.shape[2]
    every = n_src * (slots + 1)
    out = got.reshape(every, n_cols, DH)
    stats = got[:, slots]

    def three(first):
        pieces = [stats[:, :, (first + p) * slots : (first + p + 1) * slots] for p in range(3)]
        hi, mid, lo = [piece.astype(jnp.float32) for piece in pieces]
        value = jnp.pad(hi + mid + lo, ((0, 0), (0, 0), (0, 1)))
        return value.transpose(1, 0, 2).reshape(n_cols, every)

    peak, total = three(0), three(3)
    owner = stats[:, 0, 6 * slots : 7 * slots].astype(jnp.int32)
    owner = jnp.pad(owner, ((0, 0), (0, 1)), constant_values=-1).reshape(every)
    hot = owner[None, :] == jnp.arange(requests, dtype=jnp.int32)[:, None]
    masked = jnp.where(hot[None], peak[:, None, :], far_below)
    top = jnp.max(masked, axis=-1, keepdims=True)
    weight = jnp.where(hot[None], jnp.exp(masked - top), 0.0)
    den = jnp.sum(weight * total[:, None], axis=-1, keepdims=True)
    w_hi = lax.reduce_precision(weight, 8, 7)
    w_lo = (weight - w_hi).astype(jnp.bfloat16)
    w_hi = w_hi.astype(jnp.bfloat16)
    num = jnp.einsum("crj,jcd->crd", w_hi, out, preferred_element_type=jnp.float32) + jnp.einsum(
        "crj,jcd->crd", w_lo, out, preferred_element_type=jnp.float32
    )
    some = den > 0.0
    safe = jnp.where(some, den, 1.0)
    return num / safe, jnp.where(some, top + jnp.log(safe), far_below)


def fresh_kernel(kv, q_ref, keys_ref, values_ref, out_ref):
    n_steps, own_rows, width = q_ref.shape
    n_heads = width // DH
    lane = lax.broadcasted_iota(jnp.int32, (own_rows, DH), 1)
    levels = jnp.zeros((own_rows, DH), jnp.float32)
    for s in range(n_steps):
        for h in range(n_heads):
            c = s * n_heads + h
            query = q_ref[s, :, h * DH : (h + 1) * DH].astype(jnp.float32)
            fresh = [
                jnp.sum(query * keys_ref[j].astype(jnp.float32), axis=1, keepdims=True) * SCALE
                for j in range(s + 1)
            ]
            top = fresh[0]
            for x in fresh[1:]:
                top = jnp.maximum(top, x)
            num = jnp.zeros((own_rows, DH), jnp.float32)
            den = jnp.zeros((own_rows, 1), jnp.float32)
            for j in range(s + 1):
                weight = jnp.exp(fresh[j] - top)
                num = num + weight * values_ref[j].astype(jnp.float32)
                den = den + weight
            out_ref[c] = num / den
            levels = jnp.where(lane == c, top + jnp.log(den), levels)
    out_ref[n_steps * n_heads] = levels


def fresh_part(kv, queries, new_keys, new_values):
    n_steps, own_rows, width = queries.shape
    shape = (n_steps * (width // DH) + 1, own_rows, DH)
    own_kv = pl.BlockSpec((n_steps, own_rows, DH), lambda i, kv: (0, 0, kv[0]))
    return pl.pallas_call(
        fresh_kernel,
        out_shape=jax.ShapeDtypeStruct(shape, jnp.float32),
        grid_spec=pltpu.PrefetchScalarGridSpec(
            num_scalar_prefetch=1,
            grid=(1,),
            in_specs=[pl.BlockSpec(queries.shape, lambda i, kv: (0, 0, 0)), own_kv, own_kv],
            out_specs=pl.BlockSpec(shape, lambda i, kv: (0, 0, 0)),
        ),
        cost_estimate=pl.CostEstimate(flops=1 << 17, bytes_accessed=1 << 16, transcendentals=1 << 8),
        name="fresh",
    )(kv, queries, new_keys, new_values)


def finish_kernel(got, fresh, out_ref):
    n_steps, own_rows, width = out_ref.shape
    n_heads = width // DH
    last = n_steps * n_heads
    parts = [got.at[i] for i in range(got.shape[0])] + [fresh]
    levels = [part[last] for part in parts]
    top = levels[0]
    for x in levels[1:]:
        top = jnp.maximum(top, x)
    weights = [jnp.exp(x - top) for x in levels]
    den = weights[0]
    for x in weights[1:]:
        den = den + x
    inverse = 1.0 / den
    weights = [x * inverse for x in weights]
    for s in range(n_steps):
        for h in range(n_heads):
            c = s * n_heads + h
            num = jnp.zeros((own_rows, DH), jnp.float32)
            for weight, part in zip(weights, parts):
                num = num + weight[:, c : c + 1] * part[c]
            out_ref[s, :, h * DH : (h + 1) * DH] = num.astype(out_ref.dtype)


def finish(got, fresh, n_steps):
    own_rows = got.shape[2]
    width = (got.shape[1] - 1) // n_steps * DH
    return pl.pallas_call(
        finish_kernel,
        out_shape=jax.ShapeDtypeStruct((n_steps, own_rows, width), jnp.bfloat16),
        in_specs=[pl.BlockSpec(memory_space=pltpu.VMEM)] * 2,
        out_specs=pl.BlockSpec(memory_space=pltpu.VMEM),
        name="finish",
    )(got, fresh)


def body(queries, new_keys, new_values, k_cache, v_cache, block_req, block_fill):
    n_steps, own_rows, width = queries.shape
    own_heads = width // DH
    n_y, n_core = lax.axis_size("y"), lax.axis_size("core")
    n_z, n_x = lax.axis_size("z"), lax.axis_size("x")
    n_inst = n_y * n_core

    def from_other(value, axis, m):
        return lax.ppermute(value, axis, [(j, j ^ m) for j in range(lax.axis_size(axis))])

    rows = queries.reshape(n_steps, own_rows, own_heads, DH).transpose(1, 0, 2, 3)
    rows = rows.reshape(own_rows, n_steps * own_heads, DH)
    own = lax.all_to_all(
        jnp.broadcast_to(rows[None], (n_z * n_x,) + rows.shape), ("z", "x"), 0, 0, tiled=True
    )
    pieces = [own] + [from_other(own, "y", m) for m in range(n_y - 1, 0, -1)]
    pieces = pieces + [from_other(p, "core", 1) for p in pieces]
    sent = blocks(pieces, k_cache, v_cache, block_req, block_fill, n_z * n_x)
    kv = lax.axis_index("z").astype(jnp.int32).reshape(1)
    sent, kv = lax.optimization_barrier((sent, kv))
    got = lax.all_to_all(sent, ("z", "x"), split_axis=0, concat_axis=0, tiled=True)
    got, fresh = lax.optimization_barrier((got, fresh_part(kv, queries, new_keys, new_values)))
    part, level = combine(got, n_inst * own_rows)
    level = level[..., 0].reshape(4, n_inst, own_rows).transpose(1, 2, 0)
    level = jnp.pad(level, ((0, 0), (0, 0), (0, DH - 4)))[:, None]
    part = part.reshape(4, n_inst, own_rows, DH).transpose(1, 0, 2, 3)
    both = lax.all_to_all(
        jnp.concatenate([part, level], axis=1), ("y", "core"), 0, 0, tiled=True
    )
    return finish(both, fresh, n_steps)


def solution(mesh):
    n_inst, n_tp = mesh.devices.shape
    split = Mesh(
        mesh.devices.reshape(n_inst // 2, 2, KVH, n_tp // KVH), ("y", "core", "z", "x")
    )
    inst, tp = ("y", "core"), ("z", "x")
    return jax.shard_map(
        body,
        mesh=split,
        in_specs=(
            P(None, inst, tp),
            P(None, inst, None),
            P(None, inst, None),
            P(inst + tp, None, None),
            P(inst + tp, None, None),
            P(inst + tp),
            P(inst + tp),
        ),
        out_specs=P(None, inst, tp),
        check_vma=False,
    )
```

```python
import math
import jax
import jax.numpy as jnp
from jax import lax
from jax.experimental import pallas as pl
from jax.experimental.pallas import tpu as pltpu
from jax.sharding import Mesh, PartitionSpec as P

H = 64
KVH = 8
DH = 128
BLK = 128
SCALE = DH ** (-0.5)

far_below = -1e30


def split_three(x):
    hi = x.astype(jnp.bfloat16)
    rest = x - hi.astype(jnp.float32)
    mid = rest.astype(jnp.bfloat16)
    lo = (rest - mid.astype(jnp.float32)).astype(jnp.bfloat16)
    return hi, mid, lo


def hold_kernel(*refs):
    n = len(refs) // 2
    copies = [
        pltpu.make_async_copy(refs[i], refs[n + i], refs[-1].at[i]) for i in range(n)
    ]
    for c in copies:
        c.start()
    for c in copies:
        c.wait()


def hold(*arrays):
    size = sum(x.size * x.dtype.itemsize for x in arrays)
    return pl.pallas_call(
        hold_kernel,
        out_shape=[jax.ShapeDtypeStruct(x.shape, x.dtype) for x in arrays],
        in_specs=[pl.BlockSpec(memory_space=pl.ANY)] * len(arrays),
        out_specs=[pl.BlockSpec(memory_space=pl.ANY)] * len(arrays),
        scratch_shapes=[pltpu.SemaphoreType.DMA((len(arrays),))],
        compiler_params=pltpu.CompilerParams(vmem_limit_bytes=44 * 1024 * 1024),
        cost_estimate=pl.CostEstimate(flops=0, bytes_accessed=2 * size, transcendentals=0),
        name="hold",
    )(*arrays)


def block_kernel(meta, k_all, v_all, *refs):
    pieces = refs[:-4]
    out_ref, picked, stats, sem = refs[-4:]
    slots, n_tp, depth, _ = picked.shape
    cols = n_tp * depth
    n_kv = KVH
    per, n_x = cols // n_kv, n_tp // n_kv
    together = 4
    rows = pieces[0].shape[1]
    n_core = 2
    n_y = len(pieces) // n_core
    here_y, here_core = lax.axis_index("y"), lax.axis_index("core")

    def fetch(b):
        home = meta[b] // rows
        row = lax.rem(meta[b], rows)
        away = home // n_core ^ here_y
        which = away + (lax.rem(home, n_core) ^ here_core) * n_y
        for p, piece in enumerate(pieces):

            @pl.when(which == p)
            def _(piece=piece):
                pltpu.make_async_copy(piece.at[:, row], picked.at[b], sem.at[b]).start()

    def start(b, _):
        fetch(b)
        return 0

    groups = slots // together
    lax.fori_loop(0, slots, start, 0)
    stats[...] = jnp.zeros_like(stats)
    slot_at = lax.broadcasted_iota(jnp.int32, (BLK, cols), 0)
    head = lax.broadcasted_iota(jnp.int32, (DH, cols), 1) // per

    def score(b):
        query = picked[b].reshape(cols, DH).T
        nothing = jnp.zeros_like(query)
        spread = [jnp.where(head == g, query, nothing) for g in range(n_kv)]
        scores = jnp.dot(
            k_all[b], jnp.concatenate(spread, axis=0), preferred_element_type=jnp.float32
        )
        return jnp.where(slot_at < meta[slots + b], scores, far_below)

    def soften(b, scores):
        peak = jnp.max(scores, axis=0, keepdims=True)
        chances = jnp.exp2((scores - peak) * (SCALE * math.log2(math.e)))
        total = jnp.sum(chances, axis=0, keepdims=True)
        for p, piece in enumerate(split_three(peak * SCALE) + split_three(total)):
            stats[pl.ds(p * slots + b, 1)] = piece.astype(jnp.float32)
        stats[pl.ds(6 * slots + b, 1)] = jnp.broadcast_to(meta[b].astype(jnp.float32), (1, cols))
        return chances.astype(jnp.bfloat16).T

    def mix(b, rounded):
        mixed = []
        for g in range(0, n_kv, 2):
            two = jnp.dot(
                rounded[g * per : (g + 2) * per],
                v_all[b, :, g * DH : (g + 2) * DH],
                preferred_element_type=jnp.float32,
            ).astype(jnp.bfloat16)
            mixed = mixed + [two[:per, :DH], two[per:, DH:]]
        mixed = jnp.concatenate(mixed, axis=0)
        out_ref[:, pl.ds(b, 1)] = mixed.reshape(n_tp, 1, cols // n_tp, DH)

    def weigh(first):
        for j in range(together):
            pltpu.make_async_copy(pieces[0].at[:, 0], picked.at[first + j], sem.at[first + j]).wait()
        scores = [score(first + j) for j in range(together)]
        return tuple(soften(first + j, scores[j]) for j in range(together))

    def step(i, rounded):
        first = i * together
        later = weigh(first + together)
        for j in range(together):
            mix(first + j, rounded[j])
        return later

    rounded = lax.fori_loop(0, groups - 1, step, weigh(0))
    for j in range(together):
        mix(slots - together + j, rounded[j])
    packed = stats[...].T.astype(jnp.bfloat16)
    out_ref[:, pl.ds(slots, 1)] = packed.reshape(n_tp, 1, cols // n_tp, DH)


def blocks(pieces, k_cache, v_cache, meta, n_tp):
    slots = k_cache.shape[0]
    cols = n_tp * pieces[0].shape[2]
    return pl.pallas_call(
        block_kernel,
        out_shape=jax.ShapeDtypeStruct((n_tp, slots + 1, cols // n_tp, DH), jnp.bfloat16),
        in_specs=[pl.BlockSpec(memory_space=pltpu.SMEM)]
        + [pl.BlockSpec(memory_space=pltpu.VMEM)] * 2
        + [pl.BlockSpec(memory_space=pl.ANY)] * len(pieces),
        out_specs=pl.BlockSpec(memory_space=pltpu.VMEM),
        scratch_shapes=[
            pltpu.VMEM((slots,) + pieces[0].shape[:1] + pieces[0].shape[2:], pieces[0].dtype),
            pltpu.VMEM((DH, cols), jnp.float32),
            pltpu.SemaphoreType.DMA((slots,)),
        ],
        compiler_params=pltpu.CompilerParams(vmem_limit_bytes=24 * 1024 * 1024),
        cost_estimate=pl.CostEstimate(
            flops=4 * slots * BLK * DH * 128, bytes_accessed=9 * 1024 * 1024, transcendentals=slots * BLK * 128
        ),
        name="blocks",
    )(meta, k_cache, v_cache, *pieces)


def combine(got, requests):
    n_src = got.shape[0]
    slots = got.shape[1] - 1
    n_cols = got.shape[2]
    every = n_src * (slots + 1)
    out = got.reshape(every, n_cols, DH)
    stats = got[:, slots]

    def three(first):
        pieces = [stats[:, :, (first + p) * slots : (first + p + 1) * slots] for p in range(3)]
        hi, mid, lo = [piece.astype(jnp.float32) for piece in pieces]
        value = jnp.pad(hi + mid + lo, ((0, 0), (0, 0), (0, 1)))
        return value.transpose(1, 0, 2).reshape(n_cols, every)

    peak, total = three(0), three(3)
    owner = stats[:, 0, 6 * slots : 7 * slots].astype(jnp.int32)
    owner = jnp.pad(owner, ((0, 0), (0, 1)), constant_values=-1).reshape(every)
    hot = owner[None, :] == jnp.arange(requests, dtype=jnp.int32)[:, None]
    masked = jnp.where(hot[None], peak[:, None, :], far_below)
    top = jnp.max(masked, axis=-1, keepdims=True)
    weight = jnp.where(hot[None], jnp.exp(masked - top), 0.0)
    den = jnp.sum(weight * total[:, None], axis=-1, keepdims=True)
    w_hi = lax.reduce_precision(weight, 8, 7)
    w_lo = (weight - w_hi).astype(jnp.bfloat16)
    w_hi = w_hi.astype(jnp.bfloat16)
    num = jnp.einsum("crj,jcd->crd", w_hi, out, preferred_element_type=jnp.float32) + jnp.einsum(
        "crj,jcd->crd", w_lo, out, preferred_element_type=jnp.float32
    )
    some = den > 0.0
    safe = jnp.where(some, den, 1.0)
    return num / safe, jnp.where(some, top + jnp.log(safe), far_below)


def fresh_kernel(q_ref, keys_ref, values_ref, out_ref):
    n_steps, own_rows, width = q_ref.shape
    n_heads = width // DH
    own_kv = pl.ds(pl.multiple_of(lax.axis_index("z") * DH, DH), DH)
    lane = lax.broadcasted_iota(jnp.int32, (own_rows, DH), 1)
    levels = jnp.zeros((own_rows, DH), jnp.float32)
    for s in range(n_steps):
        for h in range(n_heads):
            c = s * n_heads + h
            query = q_ref[s, :, h * DH : (h + 1) * DH].astype(jnp.float32)
            fresh = [
                jnp.sum(query * keys_ref[j, :, own_kv].astype(jnp.float32), axis=1, keepdims=True) * SCALE
                for j in range(s + 1)
            ]
            top = fresh[0]
            for x in fresh[1:]:
                top = jnp.maximum(top, x)
            num = jnp.zeros((own_rows, DH), jnp.float32)
            den = jnp.zeros((own_rows, 1), jnp.float32)
            for j in range(s + 1):
                weight = jnp.exp(fresh[j] - top)
                num = num + weight * values_ref[j, :, own_kv].astype(jnp.float32)
                den = den + weight
            out_ref[c] = num / den
            levels = jnp.where(lane == c, top + jnp.log(den), levels)
    out_ref[n_steps * n_heads] = levels


def fresh_part(queries, new_keys, new_values):
    n_steps, own_rows, width = queries.shape
    return pl.pallas_call(
        fresh_kernel,
        out_shape=jax.ShapeDtypeStruct((n_steps * (width // DH) + 1, own_rows, DH), jnp.float32),
        in_specs=[pl.BlockSpec(memory_space=pltpu.VMEM)] * 3,
        out_specs=pl.BlockSpec(memory_space=pltpu.VMEM),
        cost_estimate=pl.CostEstimate(flops=1 << 17, bytes_accessed=1 << 16, transcendentals=1 << 8),
        name="fresh",
    )(queries, new_keys, new_values)


def finish_kernel(got, fresh, out_ref):
    n_steps, own_rows, width = out_ref.shape
    n_heads = width // DH
    last = n_steps * n_heads
    parts = [got.at[i] for i in range(got.shape[0])] + [fresh]
    levels = [part[last] for part in parts]
    top = levels[0]
    for x in levels[1:]:
        top = jnp.maximum(top, x)
    weights = [jnp.exp(x - top) for x in levels]
    den = weights[0]
    for x in weights[1:]:
        den = den + x
    inverse = 1.0 / den
    weights = [x * inverse for x in weights]
    for s in range(n_steps):
        for h in range(n_heads):
            c = s * n_heads + h
            num = jnp.zeros((own_rows, DH), jnp.float32)
            for weight, part in zip(weights, parts):
                num = num + weight[:, c : c + 1] * part[c]
            out_ref[s, :, h * DH : (h + 1) * DH] = num.astype(out_ref.dtype)


def finish(got, fresh, n_steps):
    own_rows = got.shape[2]
    width = (got.shape[1] - 1) // n_steps * DH
    return pl.pallas_call(
        finish_kernel,
        out_shape=jax.ShapeDtypeStruct((n_steps, own_rows, width), jnp.bfloat16),
        in_specs=[pl.BlockSpec(memory_space=pltpu.VMEM)] * 2,
        out_specs=pl.BlockSpec(memory_space=pltpu.VMEM),
        name="finish",
    )(got, fresh)


def body(queries, new_keys, new_values, k_cache, v_cache, block_req, block_fill):
    n_steps, own_rows, width = queries.shape
    own_heads = width // DH
    n_y, n_core = lax.axis_size("y"), lax.axis_size("core")
    n_z, n_x = lax.axis_size("z"), lax.axis_size("x")
    n_inst = n_y * n_core

    def from_other(value, axis, m):
        return lax.ppermute(value, axis, [(j, j ^ m) for j in range(lax.axis_size(axis))])

    rows = queries.reshape(n_steps, own_rows, own_heads, DH).transpose(1, 0, 2, 3)
    rows = rows.reshape(own_rows, n_steps * own_heads, DH)
    own = lax.all_to_all(
        jnp.broadcast_to(rows[None], (n_z * n_x,) + rows.shape), ("z", "x"), 0, 0, tiled=True
    )
    pieces = [own] + [from_other(own, "y", m) for m in range(1, n_y)]
    held, keys, values = hold(own, k_cache, v_cache)
    others, keys, values = lax.optimization_barrier((pieces[1:], keys, values))
    pieces = [own] + others
    pieces = pieces + [from_other(p, "core", 1) for p in pieces]
    meta = jnp.concatenate([block_req, block_fill])
    sent = blocks([held] + pieces[1:], keys, values, meta, n_z * n_x)
    sent, late_queries = lax.optimization_barrier((sent, queries))
    got = lax.all_to_all(sent, ("z", "x"), split_axis=0, concat_axis=0, tiled=True)
    got, fresh = lax.optimization_barrier((got, fresh_part(late_queries, new_keys, new_values)))
    part, level = combine(got, n_inst * own_rows)
    level = level[..., 0].reshape(4, n_inst, own_rows).transpose(1, 2, 0)
    level = jnp.pad(level, ((0, 0), (0, 0), (0, DH - 4)))[:, None]
    part = part.reshape(4, n_inst, own_rows, DH).transpose(1, 0, 2, 3)
    both = lax.all_to_all(
        jnp.concatenate([part, level], axis=1), ("y", "core"), 0, 0, tiled=True
    )
    return finish(both, fresh, n_steps)


def solution(mesh):
    n_inst, n_tp = mesh.devices.shape
    split = Mesh(
        mesh.devices.reshape(n_inst // 2, 2, KVH, n_tp // KVH), ("y", "core", "z", "x")
    )
    inst, tp = ("y", "core"), ("z", "x")
    return jax.shard_map(
        body,
        mesh=split,
        in_specs=(
            P(None, inst, tp),
            P(None, inst, None),
            P(None, inst, None),
            P(inst + tp, None, None),
            P(inst + tp, None, None),
            P(inst + tp),
            P(inst + tp),
        ),
        out_specs=P(None, inst, tp),
        check_vma=False,
    )
```

```python
import math
import jax
import jax.numpy as jnp
from jax import lax
from jax.experimental import pallas as pl
from jax.experimental.pallas import tpu as pltpu
from jax.sharding import Mesh, PartitionSpec as P

H = 64
KVH = 8
DH = 128
BLK = 128
SCALE = DH ** (-0.5)

far_below = -1e30


def split_three(x):
    hi = x.astype(jnp.bfloat16)
    rest = x - hi.astype(jnp.float32)
    mid = rest.astype(jnp.bfloat16)
    lo = (rest - mid.astype(jnp.float32)).astype(jnp.bfloat16)
    return hi, mid, lo


def hold_kernel(*refs):
    n = len(refs) // 2
    copies = [
        pltpu.make_async_copy(refs[i], refs[n + i], refs[-1].at[i]) for i in range(n)
    ]
    for c in copies:
        c.start()
    for c in copies:
        c.wait()


def hold(*arrays):
    size = sum(x.size * x.dtype.itemsize for x in arrays)
    return pl.pallas_call(
        hold_kernel,
        out_shape=[jax.ShapeDtypeStruct(x.shape, x.dtype) for x in arrays],
        in_specs=[pl.BlockSpec(memory_space=pl.ANY)] * len(arrays),
        out_specs=[pl.BlockSpec(memory_space=pl.ANY)] * len(arrays),
        scratch_shapes=[pltpu.SemaphoreType.DMA((len(arrays),))],
        compiler_params=pltpu.CompilerParams(vmem_limit_bytes=44 * 1024 * 1024),
        cost_estimate=pl.CostEstimate(flops=0, bytes_accessed=2 * size, transcendentals=0),
        name="hold",
    )(*arrays)


def block_kernel(meta, k_all, v_all, *refs):
    pieces = refs[:-4]
    out_ref, picked, stats, sem = refs[-4:]
    slots, n_tp, depth, _ = picked.shape
    cols = n_tp * depth
    n_kv = KVH
    per, n_x = cols // n_kv, n_tp // n_kv
    together = 4
    rows = pieces[0].shape[1]
    n_y, row_bits = len(pieces) // 2, rows.bit_length() - 1
    here_y, here_core = lax.axis_index("y"), lax.axis_index("core")

    def fetch(b):
        home = meta[b] >> row_bits
        row = meta[b] & (rows - 1)
        which = (home >> 1 ^ here_y) + (home & 1 ^ here_core) * n_y

        def choose(first, last):
            if last - first == 1:
                pltpu.make_async_copy(pieces[first].at[:, row], picked.at[b], sem.at[b]).start()
                return 0
            middle = (first + last) // 2
            return lax.cond(
                which < middle, lambda: choose(first, middle), lambda: choose(middle, last)
            )

        choose(0, len(pieces))

    def start(b, _):
        fetch(b)
        return 0

    groups = slots // together
    lax.fori_loop(0, slots, start, 0)
    stats[...] = jnp.zeros_like(stats)
    slot_at = lax.broadcasted_iota(jnp.int32, (BLK, cols), 0)
    head = lax.broadcasted_iota(jnp.int32, (DH, cols), 1) // per

    def score(b):
        query = picked[b].reshape(cols, DH).T
        nothing = jnp.zeros_like(query)
        spread = [jnp.where(head == g, query, nothing) for g in range(n_kv)]
        scores = jnp.dot(
            k_all[b], jnp.concatenate(spread, axis=0), preferred_element_type=jnp.float32
        )
        return jnp.where(slot_at < meta[slots + b], scores, far_below)

    def soften(b, scores):
        peak = jnp.max(scores, axis=0, keepdims=True)
        chances = jnp.exp2((scores - peak) * (SCALE * math.log2(math.e)))
        total = jnp.sum(chances, axis=0, keepdims=True)
        for p, piece in enumerate(split_three(peak * SCALE) + split_three(total)):
            stats[pl.ds(p * slots + b, 1)] = piece.astype(jnp.float32)
        stats[pl.ds(6 * slots + b, 1)] = jnp.broadcast_to(meta[b].astype(jnp.float32), (1, cols))
        return chances.astype(jnp.bfloat16).T

    def mix(b, rounded):
        mixed = []
        for g in range(0, n_kv, 2):
            two = jnp.dot(
                rounded[g * per : (g + 2) * per],
                v_all[b, :, g * DH : (g + 2) * DH],
                preferred_element_type=jnp.float32,
            ).astype(jnp.bfloat16)
            mixed = mixed + [two[:per, :DH], two[per:, DH:]]
        mixed = jnp.concatenate(mixed, axis=0)
        out_ref[:, pl.ds(b, 1)] = mixed.reshape(n_tp, 1, cols // n_tp, DH)

    def weigh(first):
        for j in range(together):
            pltpu.make_async_copy(pieces[0].at[:, 0], picked.at[first + j], sem.at[first + j]).wait()
        scores = [score(first + j) for j in range(together)]
        return tuple(soften(first + j, scores[j]) for j in range(together))

    def step(i, rounded):
        first = i * together
        later = weigh(first + together)
        for j in range(together):
            mix(first + j, rounded[j])
        return later

    rounded = lax.fori_loop(0, groups - 1, step, weigh(0))
    for j in range(together):
        mix(slots - together + j, rounded[j])
    packed = stats[...].T.astype(jnp.bfloat16)
    out_ref[:, pl.ds(slots, 1)] = packed.reshape(n_tp, 1, cols // n_tp, DH)


def blocks(pieces, k_cache, v_cache, meta, n_tp):
    slots = k_cache.shape[0]
    cols = n_tp * pieces[0].shape[2]
    return pl.pallas_call(
        block_kernel,
        out_shape=jax.ShapeDtypeStruct((n_tp, slots + 1, cols // n_tp, DH), jnp.bfloat16),
        in_specs=[pl.BlockSpec(memory_space=pltpu.SMEM)]
        + [pl.BlockSpec(memory_space=pltpu.VMEM)] * 2
        + [pl.BlockSpec(memory_space=pl.ANY)] * len(pieces),
        out_specs=pl.BlockSpec(memory_space=pltpu.VMEM),
        scratch_shapes=[
            pltpu.VMEM((slots,) + pieces[0].shape[:1] + pieces[0].shape[2:], pieces[0].dtype),
            pltpu.VMEM((DH, cols), jnp.float32),
            pltpu.SemaphoreType.DMA((slots,)),
        ],
        compiler_params=pltpu.CompilerParams(vmem_limit_bytes=24 * 1024 * 1024),
        cost_estimate=pl.CostEstimate(
            flops=4 * slots * BLK * DH * 128, bytes_accessed=9 * 1024 * 1024, transcendentals=slots * BLK * 128
        ),
        name="blocks",
    )(meta, k_cache, v_cache, *pieces)


def combine(got, requests):
    n_src = got.shape[0]
    slots = got.shape[1] - 1
    n_cols = got.shape[2]
    every = n_src * (slots + 1)
    out = got.reshape(every, n_cols, DH)
    stats = got[:, slots]

    def three(first):
        pieces = [stats[:, :, (first + p) * slots : (first + p + 1) * slots] for p in range(3)]
        hi, mid, lo = [piece.astype(jnp.float32) for piece in pieces]
        value = jnp.pad(hi + mid + lo, ((0, 0), (0, 0), (0, 1)))
        return value.transpose(1, 0, 2).reshape(n_cols, every)

    peak, total = three(0), three(3)
    owner = stats[:, 0, 6 * slots : 7 * slots].astype(jnp.int32)
    owner = jnp.pad(owner, ((0, 0), (0, 1)), constant_values=-1).reshape(every)
    hot = owner[None, :] == jnp.arange(requests, dtype=jnp.int32)[:, None]
    masked = jnp.where(hot[None], peak[:, None, :], far_below)
    top = jnp.max(masked, axis=-1, keepdims=True)
    weight = jnp.where(hot[None], jnp.exp(masked - top), 0.0)
    den = jnp.sum(weight * total[:, None], axis=-1, keepdims=True)
    w_hi = lax.reduce_precision(weight, 8, 7)
    w_lo = (weight - w_hi).astype(jnp.bfloat16)
    w_hi = w_hi.astype(jnp.bfloat16)
    num = jnp.einsum("crj,jcd->crd", w_hi, out, preferred_element_type=jnp.float32) + jnp.einsum(
        "crj,jcd->crd", w_lo, out, preferred_element_type=jnp.float32
    )
    some = den > 0.0
    safe = jnp.where(some, den, 1.0)
    return num / safe, jnp.where(some, top + jnp.log(safe), far_below)


def fresh_kernel(q_ref, keys_ref, values_ref, out_ref):
    n_steps, own_rows, width = q_ref.shape
    n_heads = width // DH
    own_kv = pl.ds(pl.multiple_of(lax.axis_index("z") * DH, DH), DH)
    lane = lax.broadcasted_iota(jnp.int32, (own_rows, DH), 1)
    levels = jnp.zeros((own_rows, DH), jnp.float32)
    for s in range(n_steps):
        for h in range(n_heads):
            c = s * n_heads + h
            query = q_ref[s, :, h * DH : (h + 1) * DH].astype(jnp.float32)
            fresh = [
                jnp.sum(query * keys_ref[j, :, own_kv].astype(jnp.float32), axis=1, keepdims=True) * SCALE
                for j in range(s + 1)
            ]
            top = fresh[0]
            for x in fresh[1:]:
                top = jnp.maximum(top, x)
            num = jnp.zeros((own_rows, DH), jnp.float32)
            den = jnp.zeros((own_rows, 1), jnp.float32)
            for j in range(s + 1):
                weight = jnp.exp(fresh[j] - top)
                num = num + weight * values_ref[j, :, own_kv].astype(jnp.float32)
                den = den + weight
            out_ref[c] = num / den
            levels = jnp.where(lane == c, top + jnp.log(den), levels)
    out_ref[n_steps * n_heads] = levels


def fresh_part(queries, new_keys, new_values):
    n_steps, own_rows, width = queries.shape
    return pl.pallas_call(
        fresh_kernel,
        out_shape=jax.ShapeDtypeStruct((n_steps * (width // DH) + 1, own_rows, DH), jnp.float32),
        in_specs=[pl.BlockSpec(memory_space=pltpu.VMEM)] * 3,
        out_specs=pl.BlockSpec(memory_space=pltpu.VMEM),
        cost_estimate=pl.CostEstimate(flops=1 << 17, bytes_accessed=1 << 16, transcendentals=1 << 8),
        name="fresh",
    )(queries, new_keys, new_values)


def finish_kernel(got, fresh, out_ref):
    n_steps, own_rows, width = out_ref.shape
    n_heads = width // DH
    last = n_steps * n_heads
    parts = [got.at[i] for i in range(got.shape[0])] + [fresh]
    levels = [part[last] for part in parts]
    top = levels[0]
    for x in levels[1:]:
        top = jnp.maximum(top, x)
    weights = [jnp.exp(x - top) for x in levels]
    den = weights[0]
    for x in weights[1:]:
        den = den + x
    inverse = 1.0 / den
    weights = [x * inverse for x in weights]
    for s in range(n_steps):
        for h in range(n_heads):
            c = s * n_heads + h
            num = jnp.zeros((own_rows, DH), jnp.float32)
            for weight, part in zip(weights, parts):
                num = num + weight[:, c : c + 1] * part[c]
            out_ref[s, :, h * DH : (h + 1) * DH] = num.astype(out_ref.dtype)


def finish(got, fresh, n_steps):
    own_rows = got.shape[2]
    width = (got.shape[1] - 1) // n_steps * DH
    return pl.pallas_call(
        finish_kernel,
        out_shape=jax.ShapeDtypeStruct((n_steps, own_rows, width), jnp.bfloat16),
        in_specs=[pl.BlockSpec(memory_space=pltpu.VMEM)] * 2,
        out_specs=pl.BlockSpec(memory_space=pltpu.VMEM),
        name="finish",
    )(got, fresh)


def body(queries, new_keys, new_values, k_cache, v_cache, block_req, block_fill):
    n_steps, own_rows, width = queries.shape
    own_heads = width // DH
    n_y, n_core = lax.axis_size("y"), lax.axis_size("core")
    n_z, n_x = lax.axis_size("z"), lax.axis_size("x")
    n_inst = n_y * n_core

    def from_other(value, axis, m):
        return lax.ppermute(value, axis, [(j, j ^ m) for j in range(lax.axis_size(axis))])

    rows = queries.reshape(n_steps, own_rows, own_heads, DH).transpose(1, 0, 2, 3)
    rows = rows.reshape(own_rows, n_steps * own_heads, DH)
    own = lax.all_to_all(
        jnp.broadcast_to(rows[None], (n_z * n_x,) + rows.shape), ("z", "x"), 0, 0, tiled=True
    )
    pieces = [own] + [from_other(own, "y", m) for m in range(1, n_y)]
    held, keys, values = hold(own, k_cache, v_cache)
    others, keys, values = lax.optimization_barrier((pieces[1:], keys, values))
    pieces = [own] + others
    pieces = pieces + [from_other(p, "core", 1) for p in pieces]
    meta = jnp.concatenate([block_req, block_fill])
    sent = blocks([held] + pieces[1:], keys, values, meta, n_z * n_x)
    sent, late_queries = lax.optimization_barrier((sent, queries))
    got = lax.all_to_all(sent, ("z", "x"), split_axis=0, concat_axis=0, tiled=True)
    got, fresh = lax.optimization_barrier((got, fresh_part(late_queries, new_keys, new_values)))
    part, level = combine(got, n_inst * own_rows)
    level = level[..., 0].reshape(4, n_inst, own_rows).transpose(1, 2, 0)
    level = jnp.pad(level, ((0, 0), (0, 0), (0, DH - 4)))[:, None]
    part = part.reshape(4, n_inst, own_rows, DH).transpose(1, 0, 2, 3)
    both = lax.all_to_all(
        jnp.concatenate([part, level], axis=1), ("y", "core"), 0, 0, tiled=True
    )
    return finish(both, fresh, n_steps)


def solution(mesh):
    n_inst, n_tp = mesh.devices.shape
    split = Mesh(
        mesh.devices.reshape(n_inst // 2, 2, KVH, n_tp // KVH), ("y", "core", "z", "x")
    )
    inst, tp = ("y", "core"), ("z", "x")
    return jax.shard_map(
        body,
        mesh=split,
        in_specs=(
            P(None, inst, tp),
            P(None, inst, None),
            P(None, inst, None),
            P(inst + tp, None, None),
            P(inst + tp, None, None),
            P(inst + tp),
            P(inst + tp),
        ),
        out_specs=P(None, inst, tp),
        check_vma=False,
    )
```

```python
import math
import jax
import jax.numpy as jnp
from jax import lax
from jax.experimental import pallas as pl
from jax.experimental.pallas import tpu as pltpu
from jax.sharding import Mesh, PartitionSpec as P

H = 64
KVH = 8
DH = 128
BLK = 128
SCALE = DH ** (-0.5)

far_below = -1e30


def split_three(x):
    hi = x.astype(jnp.bfloat16)
    rest = x - hi.astype(jnp.float32)
    mid = rest.astype(jnp.bfloat16)
    lo = (rest - mid.astype(jnp.float32)).astype(jnp.bfloat16)
    return hi, mid, lo


def hold_kernel(*refs):
    n = len(refs) // 2
    copies = [
        pltpu.make_async_copy(refs[i], refs[n + i], refs[-1].at[i]) for i in range(n)
    ]
    for c in copies:
        c.start()
    for c in copies:
        c.wait()


def hold(*arrays):
    size = sum(x.size * x.dtype.itemsize for x in arrays)
    return pl.pallas_call(
        hold_kernel,
        out_shape=[jax.ShapeDtypeStruct(x.shape, x.dtype) for x in arrays],
        in_specs=[pl.BlockSpec(memory_space=pl.ANY)] * len(arrays),
        out_specs=[pl.BlockSpec(memory_space=pl.ANY)] * len(arrays),
        scratch_shapes=[pltpu.SemaphoreType.DMA((len(arrays),))],
        compiler_params=pltpu.CompilerParams(vmem_limit_bytes=44 * 1024 * 1024),
        cost_estimate=pl.CostEstimate(flops=0, bytes_accessed=2 * size, transcendentals=0),
        name="hold",
    )(*arrays)


def block_kernel(meta, k_all, v_all, *refs):
    pieces = refs[:-4]
    out_ref, picked, stats, sem = refs[-4:]
    slots, n_tp, depth, _ = picked.shape
    cols = n_tp * depth
    n_kv = KVH
    per, n_x = cols // n_kv, n_tp // n_kv
    together = 8
    rows = pieces[0].shape[1]
    n_y, row_bits = len(pieces) // 2, rows.bit_length() - 1
    here_y, here_core = lax.axis_index("y"), lax.axis_index("core")

    def fetch(b):
        home = meta[b] >> row_bits
        row = meta[b] & (rows - 1)
        which = (home >> 1 ^ here_y) + (home & 1 ^ here_core) * n_y

        def choose(first, last):
            if last - first == 1:
                pltpu.make_async_copy(pieces[first].at[:, row], picked.at[b], sem.at[b]).start()
                return 0
            middle = (first + last) // 2
            return lax.cond(
                which < middle, lambda: choose(first, middle), lambda: choose(middle, last)
            )

        choose(0, len(pieces))

    def start(b, _):
        fetch(b)
        return 0

    groups = slots // together
    lax.fori_loop(0, slots, start, 0)
    stats[...] = jnp.zeros_like(stats)
    slot_at = lax.broadcasted_iota(jnp.int32, (BLK, cols), 0)
    head = lax.broadcasted_iota(jnp.int32, (DH, cols), 1) // per

    def score(b):
        query = picked[b].reshape(cols, DH).T
        nothing = jnp.zeros_like(query)
        spread = [jnp.where(head == g, query, nothing) for g in range(n_kv)]
        scores = jnp.dot(
            k_all[b], jnp.concatenate(spread, axis=0), preferred_element_type=jnp.float32
        )
        return jnp.where(slot_at < meta[slots + b], scores, far_below)

    def soften(b, scores):
        peak = jnp.max(scores, axis=0, keepdims=True)
        chances = jnp.exp2((scores - peak) * (SCALE * math.log2(math.e)))
        total = jnp.sum(chances, axis=0, keepdims=True)
        for p, piece in enumerate(split_three(peak * SCALE) + split_three(total)):
            stats[pl.ds(p * slots + b, 1)] = piece.astype(jnp.float32)
        stats[pl.ds(6 * slots + b, 1)] = jnp.broadcast_to(meta[b].astype(jnp.float32), (1, cols))
        return chances.astype(jnp.bfloat16).T

    def mix(b, rounded):
        mixed = []
        for g in range(0, n_kv, 2):
            two = jnp.dot(
                rounded[g * per : (g + 2) * per],
                v_all[b, :, g * DH : (g + 2) * DH],
                preferred_element_type=jnp.float32,
            ).astype(jnp.bfloat16)
            mixed = mixed + [two[:per, :DH], two[per:, DH:]]
        mixed = jnp.concatenate(mixed, axis=0)
        out_ref[:, pl.ds(b, 1)] = mixed.reshape(n_tp, 1, cols // n_tp, DH)

    def weigh(first):
        for j in range(together):
            pltpu.make_async_copy(pieces[0].at[:, 0], picked.at[first + j], sem.at[first + j]).wait()
        scores = [score(first + j) for j in range(together)]
        return tuple(soften(first + j, scores[j]) for j in range(together))

    def step(i, rounded):
        first = i * together
        later = weigh(first + together)
        for j in range(together):
            mix(first + j, rounded[j])
        return later

    rounded = lax.fori_loop(0, groups - 1, step, weigh(0))
    for j in range(together):
        mix(slots - together + j, rounded[j])
    packed = stats[...].T.astype(jnp.bfloat16)
    out_ref[:, pl.ds(slots, 1)] = packed.reshape(n_tp, 1, cols // n_tp, DH)


def blocks(pieces, k_cache, v_cache, meta, n_tp):
    slots = k_cache.shape[0]
    cols = n_tp * pieces[0].shape[2]
    return pl.pallas_call(
        block_kernel,
        out_shape=jax.ShapeDtypeStruct((n_tp, slots + 1, cols // n_tp, DH), jnp.bfloat16),
        in_specs=[pl.BlockSpec(memory_space=pltpu.SMEM)]
        + [pl.BlockSpec(memory_space=pltpu.VMEM)] * 2
        + [pl.BlockSpec(memory_space=pl.ANY)] * len(pieces),
        out_specs=pl.BlockSpec(memory_space=pltpu.VMEM),
        scratch_shapes=[
            pltpu.VMEM((slots,) + pieces[0].shape[:1] + pieces[0].shape[2:], pieces[0].dtype),
            pltpu.VMEM((DH, cols), jnp.float32),
            pltpu.SemaphoreType.DMA((slots,)),
        ],
        compiler_params=pltpu.CompilerParams(vmem_limit_bytes=24 * 1024 * 1024),
        cost_estimate=pl.CostEstimate(
            flops=4 * slots * BLK * DH * 128, bytes_accessed=9 * 1024 * 1024, transcendentals=slots * BLK * 128
        ),
        name="blocks",
    )(meta, k_cache, v_cache, *pieces)


def combine(got, requests):
    n_src = got.shape[0]
    slots = got.shape[1] - 1
    n_cols = got.shape[2]
    every = n_src * (slots + 1)
    out = got.reshape(every, n_cols, DH)
    stats = got[:, slots]

    def three(first):
        pieces = [stats[:, :, (first + p) * slots : (first + p + 1) * slots] for p in range(3)]
        hi, mid, lo = [piece.astype(jnp.float32) for piece in pieces]
        value = jnp.pad(hi + mid + lo, ((0, 0), (0, 0), (0, 1)))
        return value.transpose(1, 0, 2).reshape(n_cols, every)

    peak, total = three(0), three(3)
    owner = stats[:, 0, 6 * slots : 7 * slots].astype(jnp.int32)
    owner = jnp.pad(owner, ((0, 0), (0, 1)), constant_values=-1).reshape(every)
    hot = owner[None, :] == jnp.arange(requests, dtype=jnp.int32)[:, None]
    masked = jnp.where(hot[None], peak[:, None, :], far_below)
    top = jnp.max(masked, axis=-1, keepdims=True)
    weight = jnp.where(hot[None], jnp.exp(masked - top), 0.0)
    den = jnp.sum(weight * total[:, None], axis=-1, keepdims=True)
    w_hi = lax.reduce_precision(weight, 8, 7)
    w_lo = (weight - w_hi).astype(jnp.bfloat16)
    w_hi = w_hi.astype(jnp.bfloat16)
    num = jnp.einsum("crj,jcd->crd", w_hi, out, preferred_element_type=jnp.float32) + jnp.einsum(
        "crj,jcd->crd", w_lo, out, preferred_element_type=jnp.float32
    )
    some = den > 0.0
    safe = jnp.where(some, den, 1.0)
    return num / safe, jnp.where(some, top + jnp.log(safe), far_below)


def fresh_kernel(q_ref, keys_ref, values_ref, out_ref):
    n_steps, own_rows, width = q_ref.shape
    n_heads = width // DH
    own_kv = pl.ds(pl.multiple_of(lax.axis_index("z") * DH, DH), DH)
    lane = lax.broadcasted_iota(jnp.int32, (own_rows, DH), 1)
    levels = jnp.zeros((own_rows, DH), jnp.float32)
    for s in range(n_steps):
        for h in range(n_heads):
            c = s * n_heads + h
            query = q_ref[s, :, h * DH : (h + 1) * DH].astype(jnp.float32)
            fresh = [
                jnp.sum(query * keys_ref[j, :, own_kv].astype(jnp.float32), axis=1, keepdims=True) * SCALE
                for j in range(s + 1)
            ]
            top = fresh[0]
            for x in fresh[1:]:
                top = jnp.maximum(top, x)
            num = jnp.zeros((own_rows, DH), jnp.float32)
            den = jnp.zeros((own_rows, 1), jnp.float32)
            for j in range(s + 1):
                weight = jnp.exp(fresh[j] - top)
                num = num + weight * values_ref[j, :, own_kv].astype(jnp.float32)
                den = den + weight
            out_ref[c] = num / den
            levels = jnp.where(lane == c, top + jnp.log(den), levels)
    out_ref[n_steps * n_heads] = levels


def fresh_part(queries, new_keys, new_values):
    n_steps, own_rows, width = queries.shape
    return pl.pallas_call(
        fresh_kernel,
        out_shape=jax.ShapeDtypeStruct((n_steps * (width // DH) + 1, own_rows, DH), jnp.float32),
        in_specs=[pl.BlockSpec(memory_space=pltpu.VMEM)] * 3,
        out_specs=pl.BlockSpec(memory_space=pltpu.VMEM),
        cost_estimate=pl.CostEstimate(flops=1 << 17, bytes_accessed=1 << 16, transcendentals=1 << 8),
        name="fresh",
    )(queries, new_keys, new_values)


def finish_kernel(got, fresh, out_ref):
    n_steps, own_rows, width = out_ref.shape
    n_heads = width // DH
    last = n_steps * n_heads
    parts = [got.at[i] for i in range(got.shape[0])] + [fresh]
    levels = [part[last] for part in parts]
    top = levels[0]
    for x in levels[1:]:
        top = jnp.maximum(top, x)
    weights = [jnp.exp(x - top) for x in levels]
    den = weights[0]
    for x in weights[1:]:
        den = den + x
    inverse = 1.0 / den
    weights = [x * inverse for x in weights]
    for s in range(n_steps):
        for h in range(n_heads):
            c = s * n_heads + h
            num = jnp.zeros((own_rows, DH), jnp.float32)
            for weight, part in zip(weights, parts):
                num = num + weight[:, c : c + 1] * part[c]
            out_ref[s, :, h * DH : (h + 1) * DH] = num.astype(out_ref.dtype)


def finish(got, fresh, n_steps):
    own_rows = got.shape[2]
    width = (got.shape[1] - 1) // n_steps * DH
    return pl.pallas_call(
        finish_kernel,
        out_shape=jax.ShapeDtypeStruct((n_steps, own_rows, width), jnp.bfloat16),
        in_specs=[pl.BlockSpec(memory_space=pltpu.VMEM)] * 2,
        out_specs=pl.BlockSpec(memory_space=pltpu.VMEM),
        name="finish",
    )(got, fresh)


def body(queries, new_keys, new_values, k_cache, v_cache, block_req, block_fill):
    n_steps, own_rows, width = queries.shape
    own_heads = width // DH
    n_y, n_core = lax.axis_size("y"), lax.axis_size("core")
    n_z, n_x = lax.axis_size("z"), lax.axis_size("x")
    n_inst = n_y * n_core

    def from_other(value, axis, m):
        return lax.ppermute(value, axis, [(j, j ^ m) for j in range(lax.axis_size(axis))])

    rows = queries.reshape(n_steps, own_rows, own_heads, DH).transpose(1, 0, 2, 3)
    rows = rows.reshape(own_rows, n_steps * own_heads, DH)
    own = lax.all_to_all(
        jnp.broadcast_to(rows[None], (n_z * n_x,) + rows.shape), ("z", "x"), 0, 0, tiled=True
    )
    pieces = [own] + [from_other(own, "y", m) for m in range(1, n_y)]
    held, keys, values = hold(own, k_cache, v_cache)
    pieces = [own] + [lax.optimization_barrier((p, keys))[0] for p in pieces[1:]]
    pieces = pieces + [from_other(p, "core", 1) for p in pieces]
    meta = jnp.concatenate([block_req, block_fill])
    sent = blocks([held] + pieces[1:], keys, values, meta, n_z * n_x)
    sent, late_queries = lax.optimization_barrier((sent, queries))
    got = lax.all_to_all(sent, ("z", "x"), split_axis=0, concat_axis=0, tiled=True)
    got, fresh = lax.optimization_barrier((got, fresh_part(late_queries, new_keys, new_values)))
    part, level = combine(got, n_inst * own_rows)
    level = level[..., 0].reshape(4, n_inst, own_rows).transpose(1, 2, 0)
    level = jnp.pad(level, ((0, 0), (0, 0), (0, DH - 4)))[:, None]
    part = part.reshape(4, n_inst, own_rows, DH).transpose(1, 0, 2, 3)
    both = lax.all_to_all(
        jnp.concatenate([part, level], axis=1), ("y", "core"), 0, 0, tiled=True
    )
    return finish(both, fresh, n_steps)


def solution(mesh):
    n_inst, n_tp = mesh.devices.shape
    split = Mesh(
        mesh.devices.reshape(n_inst // 2, 2, KVH, n_tp // KVH), ("y", "core", "z", "x")
    )
    inst, tp = ("y", "core"), ("z", "x")
    return jax.shard_map(
        body,
        mesh=split,
        in_specs=(
            P(None, inst, tp),
            P(None, inst, None),
            P(None, inst, None),
            P(inst + tp, None, None),
            P(inst + tp, None, None),
            P(inst + tp),
            P(inst + tp),
        ),
        out_specs=P(None, inst, tp),
        check_vma=False,
    )
```

```python
import math
import jax
import jax.numpy as jnp
from jax import lax
from jax.experimental import pallas as pl
from jax.experimental.pallas import tpu as pltpu
from jax.sharding import Mesh, PartitionSpec as P

H = 64
KVH = 8
DH = 128
BLK = 128
SCALE = DH ** (-0.5)

far_below = -1e30


def split_three(x):
    hi = x.astype(jnp.bfloat16)
    rest = x - hi.astype(jnp.float32)
    mid = rest.astype(jnp.bfloat16)
    lo = (rest - mid.astype(jnp.float32)).astype(jnp.bfloat16)
    return hi, mid, lo


def hold_kernel(*refs):
    n = len(refs) // 2
    copies = [
        pltpu.make_async_copy(refs[i], refs[n + i], refs[-1].at[i]) for i in range(n)
    ]
    for c in copies:
        c.start()
    for c in copies:
        c.wait()


def hold(*arrays):
    size = sum(x.size * x.dtype.itemsize for x in arrays)
    return pl.pallas_call(
        hold_kernel,
        out_shape=[jax.ShapeDtypeStruct(x.shape, x.dtype) for x in arrays],
        in_specs=[pl.BlockSpec(memory_space=pl.ANY)] * len(arrays),
        out_specs=[pl.BlockSpec(memory_space=pl.ANY)] * len(arrays),
        scratch_shapes=[pltpu.SemaphoreType.DMA((len(arrays),))],
        compiler_params=pltpu.CompilerParams(vmem_limit_bytes=44 * 1024 * 1024),
        cost_estimate=pl.CostEstimate(flops=0, bytes_accessed=2 * size, transcendentals=0),
        name="hold",
    )(*arrays)


def block_kernel(meta, k_all, v_all, *refs):
    pieces = refs[:-4]
    out_ref, picked, stats, sem = refs[-4:]
    slots, n_tp, depth, _ = picked.shape
    cols = n_tp * depth
    n_kv = KVH
    per, n_x = cols // n_kv, n_tp // n_kv
    together = 16
    rows = pieces[0].shape[1]
    n_y, row_bits = len(pieces) // 2, rows.bit_length() - 1
    here_y, here_core = lax.axis_index("y"), lax.axis_index("core")

    def fetch(b):
        home = meta[b] >> row_bits
        row = meta[b] & (rows - 1)
        which = (home >> 1 ^ here_y) + (home & 1 ^ here_core) * n_y

        def choose(first, last):
            if last - first == 1:
                pltpu.make_async_copy(pieces[first].at[:, row], picked.at[b], sem.at[b]).start()
                return 0
            middle = (first + last) // 2
            return lax.cond(
                which < middle, lambda: choose(first, middle), lambda: choose(middle, last)
            )

        choose(0, len(pieces))

    def start(b, _):
        fetch(b)
        return 0

    groups = slots // together
    lax.fori_loop(0, slots, start, 0)
    stats[...] = jnp.zeros_like(stats)
    slot_at = lax.broadcasted_iota(jnp.int32, (BLK, cols), 0)
    head = lax.broadcasted_iota(jnp.int32, (DH, cols), 1) // per

    def score(b):
        query = picked[b].reshape(cols, DH).T
        nothing = jnp.zeros_like(query)
        spread = [jnp.where(head == g, query, nothing) for g in range(n_kv)]
        scores = jnp.dot(
            k_all[b], jnp.concatenate(spread, axis=0), preferred_element_type=jnp.float32
        )
        return jnp.where(slot_at < meta[slots + b], scores, far_below)

    def soften(b, scores):
        peak = jnp.max(scores, axis=0, keepdims=True)
        chances = jnp.exp2((scores - peak) * (SCALE * math.log2(math.e)))
        total = jnp.sum(chances, axis=0, keepdims=True)
        for p, piece in enumerate(split_three(peak * SCALE) + split_three(total)):
            stats[pl.ds(p * slots + b, 1)] = piece.astype(jnp.float32)
        stats[pl.ds(6 * slots + b, 1)] = jnp.broadcast_to(meta[b].astype(jnp.float32), (1, cols))
        return chances.astype(jnp.bfloat16).T

    def mix(b, rounded):
        mixed = []
        for g in range(0, n_kv, 2):
            two = jnp.dot(
                rounded[g * per : (g + 2) * per],
                v_all[b, :, g * DH : (g + 2) * DH],
                preferred_element_type=jnp.float32,
            ).astype(jnp.bfloat16)
            mixed = mixed + [two[:per, :DH], two[per:, DH:]]
        mixed = jnp.concatenate(mixed, axis=0)
        out_ref[:, pl.ds(b, 1)] = mixed.reshape(n_tp, 1, cols // n_tp, DH)

    def weigh(first):
        for j in range(together):
            pltpu.make_async_copy(pieces[0].at[:, 0], picked.at[first + j], sem.at[first + j]).wait()
        scores = [score(first + j) for j in range(together)]
        return tuple(soften(first + j, scores[j]) for j in range(together))

    def step(i, rounded):
        first = i * together
        later = weigh(first + together)
        for j in range(together):
            mix(first + j, rounded[j])
        return later

    rounded = weigh(0)
    if groups > 1:
        rounded = lax.fori_loop(0, groups - 1, step, rounded)
    for j in range(together):
        mix(slots - together + j, rounded[j])
    packed = stats[...].T.astype(jnp.bfloat16)
    out_ref[:, pl.ds(slots, 1)] = packed.reshape(n_tp, 1, cols // n_tp, DH)


def blocks(pieces, k_cache, v_cache, meta, n_tp):
    slots = k_cache.shape[0]
    cols = n_tp * pieces[0].shape[2]
    return pl.pallas_call(
        block_kernel,
        out_shape=jax.ShapeDtypeStruct((n_tp, slots + 1, cols // n_tp, DH), jnp.bfloat16),
        in_specs=[pl.BlockSpec(memory_space=pltpu.SMEM)]
        + [pl.BlockSpec(memory_space=pltpu.VMEM)] * 2
        + [pl.BlockSpec(memory_space=pl.ANY)] * len(pieces),
        out_specs=pl.BlockSpec(memory_space=pltpu.VMEM),
        scratch_shapes=[
            pltpu.VMEM((slots,) + pieces[0].shape[:1] + pieces[0].shape[2:], pieces[0].dtype),
            pltpu.VMEM((DH, cols), jnp.float32),
            pltpu.SemaphoreType.DMA((slots,)),
        ],
        compiler_params=pltpu.CompilerParams(vmem_limit_bytes=24 * 1024 * 1024),
        cost_estimate=pl.CostEstimate(
            flops=4 * slots * BLK * DH * 128, bytes_accessed=9 * 1024 * 1024, transcendentals=slots * BLK * 128
        ),
        name="blocks",
    )(meta, k_cache, v_cache, *pieces)


def combine(got, requests):
    n_src = got.shape[0]
    slots = got.shape[1] - 1
    n_cols = got.shape[2]
    every = n_src * (slots + 1)
    out = got.reshape(every, n_cols, DH)
    stats = got[:, slots]

    def three(first):
        pieces = [stats[:, :, (first + p) * slots : (first + p + 1) * slots] for p in range(3)]
        hi, mid, lo = [piece.astype(jnp.float32) for piece in pieces]
        value = jnp.pad(hi + mid + lo, ((0, 0), (0, 0), (0, 1)))
        return value.transpose(1, 0, 2).reshape(n_cols, every)

    peak, total = three(0), three(3)
    owner = stats[:, 0, 6 * slots : 7 * slots].astype(jnp.int32)
    owner = jnp.pad(owner, ((0, 0), (0, 1)), constant_values=-1).reshape(every)
    hot = owner[None, :] == jnp.arange(requests, dtype=jnp.int32)[:, None]
    masked = jnp.where(hot[None], peak[:, None, :], far_below)
    top = jnp.max(masked, axis=-1, keepdims=True)
    weight = jnp.where(hot[None], jnp.exp(masked - top), 0.0)
    den = jnp.sum(weight * total[:, None], axis=-1, keepdims=True)
    w_hi = lax.reduce_precision(weight, 8, 7)
    w_lo = (weight - w_hi).astype(jnp.bfloat16)
    w_hi = w_hi.astype(jnp.bfloat16)
    num = jnp.einsum("crj,jcd->crd", w_hi, out, preferred_element_type=jnp.float32) + jnp.einsum(
        "crj,jcd->crd", w_lo, out, preferred_element_type=jnp.float32
    )
    some = den > 0.0
    safe = jnp.where(some, den, 1.0)
    return num / safe, jnp.where(some, top + jnp.log(safe), far_below)


def fresh_kernel(q_ref, keys_ref, values_ref, out_ref):
    n_steps, own_rows, width = q_ref.shape
    n_heads = width // DH
    own_kv = pl.ds(pl.multiple_of(lax.axis_index("z") * DH, DH), DH)
    lane = lax.broadcasted_iota(jnp.int32, (own_rows, DH), 1)
    levels = jnp.zeros((own_rows, DH), jnp.float32)
    for s in range(n_steps):
        for h in range(n_heads):
            c = s * n_heads + h
            query = q_ref[s, :, h * DH : (h + 1) * DH].astype(jnp.float32)
            fresh = [
                jnp.sum(query * keys_ref[j, :, own_kv].astype(jnp.float32), axis=1, keepdims=True) * SCALE
                for j in range(s + 1)
            ]
            top = fresh[0]
            for x in fresh[1:]:
                top = jnp.maximum(top, x)
            num = jnp.zeros((own_rows, DH), jnp.float32)
            den = jnp.zeros((own_rows, 1), jnp.float32)
            for j in range(s + 1):
                weight = jnp.exp(fresh[j] - top)
                num = num + weight * values_ref[j, :, own_kv].astype(jnp.float32)
                den = den + weight
            out_ref[c] = num / den
            levels = jnp.where(lane == c, top + jnp.log(den), levels)
    out_ref[n_steps * n_heads] = levels


def fresh_part(queries, new_keys, new_values):
    n_steps, own_rows, width = queries.shape
    return pl.pallas_call(
        fresh_kernel,
        out_shape=jax.ShapeDtypeStruct((n_steps * (width // DH) + 1, own_rows, DH), jnp.float32),
        in_specs=[pl.BlockSpec(memory_space=pltpu.VMEM)] * 3,
        out_specs=pl.BlockSpec(memory_space=pltpu.VMEM),
        cost_estimate=pl.CostEstimate(flops=1 << 17, bytes_accessed=1 << 16, transcendentals=1 << 8),
        name="fresh",
    )(queries, new_keys, new_values)


def finish_kernel(got, fresh, out_ref):
    n_steps, own_rows, width = out_ref.shape
    n_heads = width // DH
    last = n_steps * n_heads
    parts = [got.at[i] for i in range(got.shape[0])] + [fresh]
    levels = [part[last] for part in parts]
    top = levels[0]
    for x in levels[1:]:
        top = jnp.maximum(top, x)
    weights = [jnp.exp(x - top) for x in levels]
    den = weights[0]
    for x in weights[1:]:
        den = den + x
    inverse = 1.0 / den
    weights = [x * inverse for x in weights]
    for s in range(n_steps):
        for h in range(n_heads):
            c = s * n_heads + h
            num = jnp.zeros((own_rows, DH), jnp.float32)
            for weight, part in zip(weights, parts):
                num = num + weight[:, c : c + 1] * part[c]
            out_ref[s, :, h * DH : (h + 1) * DH] = num.astype(out_ref.dtype)


def finish(got, fresh, n_steps):
    own_rows = got.shape[2]
    width = (got.shape[1] - 1) // n_steps * DH
    return pl.pallas_call(
        finish_kernel,
        out_shape=jax.ShapeDtypeStruct((n_steps, own_rows, width), jnp.bfloat16),
        in_specs=[pl.BlockSpec(memory_space=pltpu.VMEM)] * 2,
        out_specs=pl.BlockSpec(memory_space=pltpu.VMEM),
        name="finish",
    )(got, fresh)


def body(queries, new_keys, new_values, k_cache, v_cache, block_req, block_fill):
    n_steps, own_rows, width = queries.shape
    own_heads = width // DH
    n_y, n_core = lax.axis_size("y"), lax.axis_size("core")
    n_z, n_x = lax.axis_size("z"), lax.axis_size("x")
    n_inst = n_y * n_core

    def from_other(value, axis, m):
        return lax.ppermute(value, axis, [(j, j ^ m) for j in range(lax.axis_size(axis))])

    rows = queries.reshape(n_steps, own_rows, own_heads, DH).transpose(1, 0, 2, 3)
    rows = rows.reshape(own_rows, n_steps * own_heads, DH)
    own = lax.all_to_all(
        jnp.broadcast_to(rows[None], (n_z * n_x,) + rows.shape), ("z", "x"), 0, 0, tiled=True
    )
    pieces = [own] + [from_other(own, "y", m) for m in range(1, n_y)]
    held, keys, values = hold(own, k_cache, v_cache)
    pieces = [own] + [lax.optimization_barrier((p, keys))[0] for p in pieces[1:]]
    pieces = pieces + [from_other(p, "core", 1) for p in pieces]
    meta = jnp.concatenate([block_req, block_fill])
    sent = blocks([held] + pieces[1:], keys, values, meta, n_z * n_x)
    sent, late_queries = lax.optimization_barrier((sent, queries))
    got = lax.all_to_all(sent, ("z", "x"), split_axis=0, concat_axis=0, tiled=True)
    got, fresh = lax.optimization_barrier((got, fresh_part(late_queries, new_keys, new_values)))
    part, level = combine(got, n_inst * own_rows)
    level = level[..., 0].reshape(4, n_inst, own_rows).transpose(1, 2, 0)
    level = jnp.pad(level, ((0, 0), (0, 0), (0, DH - 4)))[:, None]
    part = part.reshape(4, n_inst, own_rows, DH).transpose(1, 0, 2, 3)
    both = lax.all_to_all(
        jnp.concatenate([part, level], axis=1), ("y", "core"), 0, 0, tiled=True
    )
    return finish(both, fresh, n_steps)


def solution(mesh):
    n_inst, n_tp = mesh.devices.shape
    split = Mesh(
        mesh.devices.reshape(n_inst // 2, 2, KVH, n_tp // KVH), ("y", "core", "z", "x")
    )
    inst, tp = ("y", "core"), ("z", "x")
    return jax.shard_map(
        body,
        mesh=split,
        in_specs=(
            P(None, inst, tp),
            P(None, inst, None),
            P(None, inst, None),
            P(inst + tp, None, None),
            P(inst + tp, None, None),
            P(inst + tp),
            P(inst + tp),
        ),
        out_specs=P(None, inst, tp),
        check_vma=False,
    )
```
